512 devices in a mesh: grp: 16 (over x_hi, y), dom: 32 (over z, x_lo, core).
Axes of the slice: x: 4 (x_hi: 2, x_lo: 2; x = x_hi * 2 + x_lo), y: 8, z: 8, core: 2. Of those that a mesh axis runs over, the one named last changes fastest.
Arguments:
- particles: float32 [8, 2621440], P(None, ('grp', 'dom')), may hold values from -1.2 to 707, as said below
- ghost_lists: int32 [2, 32768], P(None, ('grp', 'dom')), may hold values from 0 to 1023, as said below
- pair_lists: int32 [4, 393216], P(None, ('grp', 'dom')), may hold values from 1024 to 5119, as said below
Outputs:
- density: float32 [2621440], P(('grp', 'dom'))
- accel: float32 [3, 2621440], P(None, ('grp', 'dom'))
The draws below stay inside these ranges and needn't reach their ends.
Inputs may be any that keep to these rules, and one draw needn't show every extreme that they name: `particles`: tile t of a domain is its rows t * 64 to (t + 1) * 64 - 1; tiles 0 to 15 are its slab, then four pair regions of 16 tiles. Particles closer than 1 to each other are in the same or adjacent tiles of one domain, or in slab tiles 0 and 15 of domains adjacent along dom in one group, or in tile j of round r's region of partner domains e and e xor k_r and tiles j - 1 to j + 1 of the other. Masses and sound speeds lie in 0.5 to 2. `ghost_lists`: row 0 holds 64 distinct rows of a domain's first 128, row 1 distinct rows of its slab tiles 16 - 2 and 15. `pair_lists`: row r holds, block j after block j, 48 distinct rows of tile j of the domain's r-th pair region.
All inputs are finite; a program needn't handle non-finite values.
Results may differ from the reference program's by a relative error of at most 0.0003.
Values sent between devices are 32-bit elements; how exact they have to be, the bound alone decides.
A program may use at most 64 MiB of HBM per device.

```python
import math
import jax
import jax.numpy as jnp
from jax import lax

TILE_ROWS = 64
LISTED = 48
SLAB_TILES = 16
PAIR_TILES = 16
DOMAIN_ROWS = 5120
PARTICLES = 2621440
N_GRP = 16
N_DOM = 32


def draw_particles(key, part):
    domain_rows = TILE_ROWS * (SLAB_TILES + 4 * PAIR_TILES)
    total = domain_rows * N_GRP * N_DOM
    column = jnp.arange(total, dtype=jnp.int32)
    device = column // domain_rows
    tile = column % domain_rows // TILE_ROWS
    domain = device % N_DOM
    group = device // N_DOM
    region = jnp.clip((tile - SLAB_TILES) // PAIR_TILES, 0, 3)
    within = (tile - SLAB_TILES) % PAIR_TILES
    flip = jnp.where(region == 0, 1, jnp.where(region == 1, 4, jnp.where(region == 2, N_DOM, 2 * N_DOM)))
    lowest = jnp.minimum(device, jnp.bitwise_xor(device, flip))
    in_slab = tile < SLAB_TILES
    breadth = math.sqrt(TILE_ROWS / 12.0)
    keys = jax.random.split(key, 4)
    spot = jax.random.uniform(keys[0], (3, total), jnp.float32)
    xpos = jnp.where(in_slab, domain * SLAB_TILES + tile, within).astype(jnp.float32) + spot[0]
    ypos = jnp.where(in_slab, 8.0 * group.astype(jnp.float32), 200.0 + 8.0 * (lowest % 64).astype(jnp.float32)) + breadth * spot[1]
    zpos = jnp.where(in_slab, 0.0, 8.0 * (region + 4 * (lowest // 64)).astype(jnp.float32)) + breadth * spot[2]
    motion = 0.3 * jax.random.truncated_normal(keys[1], -4.0, 4.0, (3, total), jnp.float32)
    low_log = math.log(0.5)
    high_log = math.log(2.0)
    mass = jnp.exp(jax.random.uniform(keys[2], (total,), jnp.float32, low_log, high_log))
    sound = jnp.exp(jax.random.uniform(keys[3], (total,), jnp.float32, low_log, high_log))
    return jnp.concatenate([xpos[None], ypos[None], zpos[None], motion, mass[None], sound[None]], axis=0)


def draw_ghost_lists(key, part):
    devices = N_GRP * N_DOM
    keys = jax.random.split(key, 2 * devices)

    def choose(subkey):
        return jax.random.permutation(subkey, 2 * TILE_ROWS)[:TILE_ROWS]
    chosen = jax.vmap(choose)(keys).reshape(devices, 2, TILE_ROWS).astype(jnp.int32)
    offset = jnp.array([0, (SLAB_TILES - 2) * TILE_ROWS], jnp.int32)
    chosen = chosen + offset[None, :, None]
    return jnp.transpose(chosen, (1, 0, 2)).reshape(2, devices * TILE_ROWS)


def draw_pair_lists(key, part):
    devices = N_GRP * N_DOM
    keys = jax.random.split(key, devices * 4 * PAIR_TILES)

    def choose(subkey):
        return jax.random.permutation(subkey, TILE_ROWS)[:LISTED]
    chosen = jax.vmap(choose)(keys).reshape(devices, 4, PAIR_TILES, LISTED).astype(jnp.int32)
    tile_index = jnp.arange(4 * PAIR_TILES, dtype=jnp.int32).reshape(4, PAIR_TILES)
    base = SLAB_TILES * TILE_ROWS + tile_index * TILE_ROWS
    chosen = chosen + base[None, :, :, None]
    return jnp.transpose(chosen, (1, 0, 2, 3)).reshape(4, devices * PAIR_TILES * LISTED)


def setup_inputs(seed: int = 0) -> dict:
    arg_keys = jax.random.split(jax.random.key(seed), 4)
    return {
        "particles": draw_particles(jax.random.fold_in(arg_keys[3], 71), 0),
        "ghost_lists": draw_ghost_lists(jax.random.fold_in(arg_keys[3], 71), 0),
        "pair_lists": draw_pair_lists(jax.random.fold_in(arg_keys[3], 71), 0),
    }


rest_density = 8.0
far_value = -1000.0
filler_values = (far_value, far_value, far_value, 0.0, 0.0, 0.0, 0.0, 1.0, 1.0, 0.0)

def filler(fields, width):
    column = jnp.array(filler_values[:fields], jnp.float32)
    return jnp.broadcast_to(column[:, None, None], (fields, 1, width))

def window(tiled):
    fields, tile_count, width = tiled.shape
    padded = jnp.concatenate([filler(fields, width), tiled, filler(fields, width)], axis=1)
    return jnp.concatenate([padded[:, 0:tile_count], padded[:, 1:tile_count + 1], padded[:, 2:tile_count + 2]], axis=2)

def with_pressure(nine_rows):
    sound = nine_rows[7]
    pressure = sound * sound * (nine_rows[8] - rest_density)
    return jnp.concatenate([nine_rows, pressure[None]], axis=0)

def density_block(own_pos, other_pos, other_mass):
    offsets = own_pos[:, :, :, None] - other_pos[:, :, None, :]
    squared = offsets[0] * offsets[0] + offsets[1] * offsets[1] + offsets[2] * offsets[2]
    softer = 1.0 - squared
    weight = jnp.where(squared < 1.0, softer * softer * softer, 0.0)
    return (lax.optimization_barrier(jnp.sum(weight * other_mass[0][:, None, :], axis=2))[None],)

def pair_scale(own_rows, other_rows):
    offsets = own_rows[0:3, :, :, None] - other_rows[0:3, :, None, :]
    squared = offsets[0] * offsets[0] + offsets[1] * offsets[1] + offsets[2] * offsets[2]
    distance = jnp.sqrt(jnp.maximum(squared, 0.01))
    relative = own_rows[3:6, :, :, None] - other_rows[3:6, :, None, :]
    normal = (relative[0] * offsets[0] + relative[1] * offsets[1] + relative[2] * offsets[2]) / distance
    own_imp = (own_rows[8] * own_rows[7])[:, :, None]
    other_imp = (other_rows[8] * other_rows[7])[:, None, :]
    star = (other_imp * own_rows[9][:, :, None] + own_imp * other_rows[9][:, None, :] - own_imp * other_imp * normal) / (own_imp + other_imp)
    softer = 1.0 - squared
    scale = jnp.where(squared < 1.0, 12.0 * star * softer * softer / (own_rows[8][:, :, None] * other_rows[8][:, None, :]), 0.0)
    return (offsets, scale)

def own_gain(own_rows, other_rows):
    offsets, scale = pair_scale(own_rows, other_rows)
    return lax.optimization_barrier(jnp.sum((scale * other_rows[6][:, None, :])[None] * offsets, axis=3))

def rows_of(array, device, width):
    return lax.dynamic_slice_in_dim(array, device * width, width, axis=1)

def reference(particles, ghost_lists, pair_lists):
    devices = N_GRP * N_DOM
    tile_count = DOMAIN_ROWS // TILE_ROWS
    pair_rows = LISTED * PAIR_TILES
    face = 2 * TILE_ROWS
    top = SLAB_TILES * TILE_ROWS
    masks = (1, 4, N_DOM, 2 * N_DOM)

    def density_of(device):
        own = rows_of(particles, device, DOMAIN_ROWS)
        tiled = own.reshape(8, tile_count, TILE_ROWS)
        beside_all = window(tiled)
        density = density_block(tiled[0:3], beside_all[0:3], beside_all[6:7])[0].reshape(DOMAIN_ROWS)
        domain = device % N_DOM
        lower = jnp.maximum(device - 1, 0)
        upper = jnp.minimum(device + 1, devices - 1)
        from_lower = jnp.take(rows_of(particles, lower, DOMAIN_ROWS), rows_of(ghost_lists, lower, TILE_ROWS)[1], axis=1)
        from_upper = jnp.take(rows_of(particles, upper, DOMAIN_ROWS), rows_of(ghost_lists, upper, TILE_ROWS)[0], axis=1)
        lower_mass = from_lower[6:7] * (domain > 0).astype(jnp.float32)
        upper_mass = from_upper[6:7] * (domain < N_DOM - 1).astype(jnp.float32)
        density = density.at[0:face].add(density_block(own[0:3, None, 0:face], from_lower[0:3, None, :], lower_mass[:, None, :])[0][0, 0])
        density = density.at[top - face:top].add(density_block(own[0:3, None, top - face:top], from_upper[0:3, None, :], upper_mass[:, None, :])[0][0, 0])
        for round_index in range(4):
            partner = jnp.bitwise_xor(device, masks[round_index]).astype(jnp.int32)
            chosen = rows_of(pair_lists, device, pair_rows)[round_index]
            their_chosen = rows_of(pair_lists, partner, pair_rows)[round_index]
            mine = jnp.take(own, chosen, axis=1)[0:3].reshape(3, PAIR_TILES, LISTED)
            theirs_all = jnp.take(rows_of(particles, partner, DOMAIN_ROWS), their_chosen, axis=1)
            theirs = jnp.concatenate([theirs_all[0:3], theirs_all[6:7]], axis=0).reshape(4, PAIR_TILES, LISTED)
            near = window(theirs)
            density = density.at[chosen].add(density_block(mine, near[0:3], near[3:4])[0].reshape(pair_rows))
        return density
    density_all = lax.map(density_of, jnp.arange(devices, dtype=jnp.int32))

    def extended_of(which):
        return with_pressure(jnp.concatenate([rows_of(particles, which, DOMAIN_ROWS), density_all[which][None]], axis=0))

    def force_of(device):
        extended = extended_of(device)
        tiled = extended.reshape(10, tile_count, TILE_ROWS)
        accel = own_gain(tiled, window(tiled)).reshape(3, DOMAIN_ROWS)
        for round_index in range(4):
            partner = jnp.bitwise_xor(device, masks[round_index]).astype(jnp.int32)
            chosen = rows_of(pair_lists, device, pair_rows)[round_index]
            their_chosen = rows_of(pair_lists, partner, pair_rows)[round_index]
            mine = jnp.take(extended, chosen, axis=1).reshape(10, PAIR_TILES, LISTED)
            theirs = jnp.take(extended_of(partner), their_chosen, axis=1).reshape(10, PAIR_TILES, LISTED)
            accel = accel.at[:, chosen].add(own_gain(mine, window(theirs)).reshape(3, pair_rows))
        return accel
    accel_all = lax.map(force_of, jnp.arange(devices, dtype=jnp.int32))
    return (density_all.reshape(PARTICLES), jnp.transpose(accel_all, (1, 0, 2)).reshape(3, PARTICLES))
```

```python
import jax
import jax.numpy as jnp
from jax import lax
from jax.experimental import pallas as pl
from jax.experimental.pallas import tpu as pltpu
from jax.sharding import PartitionSpec as P

F32 = jnp.float32
REST = 8.0
FAR = -1000.0
LANES = 128
MESH = pl.DeviceIdType.MESH

WALKS = ((0, 4, 0, 4), (10, 8, 8, 16), (28, 8, 24, 32))
SLOTS = 48
FIRST_STEP = (0, 8, 24)
OWN_CHUNKS = 8
LISTED_CHUNKS = 6
OWN_TERMS = 40 * 3 * OWN_CHUNKS
EDGE_TERMS = 6 * OWN_CHUNKS
LISTED_TERMS = 32 * 3 * LISTED_CHUNKS
TERMS = OWN_TERMS + EDGE_TERMS + LISTED_TERMS

ENTRIES = (0, 1, 2, 3, 4, 5, 6, 7, None, 8, 15, 16, 23, 24, 31, 32)
ENTRY = {pair: place for place, pair in enumerate(ENTRIES)}
EDGES = (((None, 3), (4, 8)), ((7, 15), (16, 24)), ((23, 31), (32, None)))


def spread(rows, lanes):
    return lax.gather(
        rows,
        lanes[:, :, None],
        lax.GatherDimensionNumbers(
            offset_dims=(),
            collapsed_slice_dims=(1,),
            start_index_map=(1,),
            operand_batching_dims=(0,),
            start_indices_batching_dims=(0,),
        ),
        slice_sizes=(1, 1),
        mode=lax.GatherScatterMode.PROMISE_IN_BOUNDS,
    )


def total(block):
    return jnp.sum(block, axis=0, keepdims=True)


def kernel(
    particles,
    ghost_lists,
    pair_lists,
    density_out,
    accel_out,
    stack,
    target,
    fields,
    given,
    theirs,
    lists,
    lists_t,
    picks,
    outgoing,
    incoming,
    ghost_out,
    ghost_in,
    dens_out,
    dens_in,
    terms,
    acc_density,
    acc_force,
    row_density,
    row_a,
    row_b,
    row_scale,
    row_member,
    row_force,
    natural,
    extra,
    theirs_given,
    send_sem,
    recv_sem,
):
    grp = lax.axis_index("grp")
    dom = lax.axis_index("dom")
    n_dom = lax.axis_size("dom")

    def flipped(value, bit):
        return value + bit - 2 * bit * (lax.rem(lax.div(value, bit), 2))

    partners = (
        (grp, flipped(dom, 1)),
        (grp, flipped(dom, 4)),
        (flipped(grp, 1), dom),
        (flipped(grp, 2), dom),
    )
    below = (grp, lax.rem(dom + n_dom - 1, n_dom))
    above = (grp, lax.rem(dom + 1, n_dom))

    barrier = pltpu.get_barrier_semaphore()
    for peer in partners + (below, above):
        pl.semaphore_signal(barrier, inc=1, device_id=peer, device_id_type=MESH)

    lane = lax.broadcasted_iota(jnp.int32, (8, LANES), 1)
    first_half = lane < 64
    half = jnp.where(first_half, 0, 1)

    def pick_half(low, high):
        return jnp.where(first_half[0 : low.shape[0]], low, high)

    def swap(block):
        return pltpu.roll(block, 64, 1)

    padded = jnp.concatenate([pair_lists[...], jnp.zeros((4, LANES), jnp.int32)], axis=1)
    padded = jnp.concatenate([padded, padded], axis=0)
    for j in range(16):
        lists[pl.ds(8 * j, 8), :] = jnp.bitwise_and(padded[:, 48 * j : 48 * j + LANES], 63)
    for k in range(8):
        even = lists[pl.ds(16 * k, 8), :]
        odd = lists[pl.ds(16 * k + 8, 8), :]
        both = pick_half(even, swap(odd) + 64)
        for r in range(4):
            picks[pl.ds(8 * r + k, 1), :] = both[r : r + 1]

    for p in range(40):
        stack[pl.ds(8 * p, 8), :] = particles[:, LANES * p : LANES * p + LANES]

    for r in range(4):
        for k in range(8):
            index = jnp.broadcast_to(picks[pl.ds(8 * r + k, 1), :], (8, LANES))
            outgoing[r, pl.ds(8 * k, 8), :] = spread(stack[pl.ds(8 * (8 + 8 * r + k), 8), :], index)
    faces = jnp.concatenate([ghost_lists[...], ghost_lists[...]], axis=1)
    for side, pair in ((0, 0), (1, 7)):
        index = jnp.broadcast_to(jnp.bitwise_and(faces[side : side + 1], 127), (8, LANES))
        ghost_out[side] = spread(stack[pl.ds(8 * pair, 8), :], index)

    pl.semaphore_wait(barrier, 6)

    def send(source, destination, number, peer):
        copy = pltpu.make_async_remote_copy(
            src_ref=source,
            dst_ref=destination,
            send_sem=send_sem.at[number],
            recv_sem=recv_sem.at[number],
            device_id=peer,
            device_id_type=MESH,
        )
        copy.start()
        return copy

    pair_copies = [
        send(outgoing.at[r], incoming.at[pl.ds(64 * r, 64)], r, partners[r]) for r in (3, 2, 1, 0)
    ]
    ghost_copies = [
        send(ghost_out.at[0], ghost_in.at[pl.ds(8, 8)], 4, below),
        send(ghost_out.at[1], ghost_in.at[pl.ds(0, 8)], 5, above),
    ]

    filler_field = lax.broadcasted_iota(jnp.int32, (8, LANES), 0)
    filler = jnp.where(filler_field < 3, FAR, 0.0).astype(F32)
    fields[0] = jnp.transpose(
        jnp.concatenate(
            [filler if pair is None else stack[pl.ds(8 * pair, 8), :] for pair in ENTRIES], axis=0
        )
    )
    fields[1] = jnp.transpose(stack[pl.ds(64, 128), :])
    fields[2] = jnp.transpose(stack[pl.ds(192, 128), :])
    lists_t[...] = jnp.transpose(lists[...].astype(F32))

    zero = jnp.zeros((8, LANES), F32)
    for base, pairs, low, high in WALKS:
        for k in range(pairs):
            one = stack[pl.ds(8 * (low + k), 8), :]
            two = stack[pl.ds(8 * (high + k), 8), :]
            target[pl.ds(8 * (base + 1 + 2 * k), 8), :] = pick_half(one, swap(two))
            target[pl.ds(8 * (base + 2 + 2 * k), 8), :] = pick_half(swap(one), two)
        target[pl.ds(8 * base, 8), :] = zero
        target[pl.ds(8 * (base + 1 + 2 * pairs), 8), :] = zero
    for slot in (46, 47):
        target[pl.ds(8 * slot, 8), :] = zero

    def meet(block, row, lanes, chunks, slots, term):
        sums = [zero for _ in slots]
        aims = [
            [
                jnp.broadcast_to(target[pl.ds(8 * slot + f, 1), :], (8, LANES))
                for f in range(6)
            ]
            for slot in slots
        ]
        for c in range(chunks):
            rows = block[pl.ds(row + 8 * c, 8), :]
            xs, ys, zs, us, vs, ws, mass = [spread(rows, lanes + f) for f in range(7)]
            for n in range(len(slots)):
                xt, yt, zt, ut, vt, wt = aims[n]
                dx, dy, dz = xt - xs, yt - ys, zt - zs
                squared = dx * dx + dy * dy + dz * dz
                near = jnp.maximum(1.0 - squared, 0.0)
                near2 = near * near
                sums[n] = sums[n] + mass * (near2 * near)
                along = (ut - us) * dx + (vt - vs) * dy + (wt - ws) * dz
                place = term + 4 * (c * len(slots) + n)
                terms[place] = along * lax.rsqrt(jnp.maximum(squared, 0.01))
                terms[place + 1] = near2 * dx
                terms[place + 2] = near2 * dy
                terms[place + 3] = near2 * dz
        return sums

    def edge_lanes(pair_low, pair_high, stride, scale):
        return jnp.where(first_half, scale * ENTRY[pair_low], scale * ENTRY[pair_high])

    def own_density(walk):
        base, pairs, low, high = WALKS[walk]
        before, after = EDGES[walk]
        block = fields.at[walk]
        span = half * (32 if walk == 0 else 64)
        edge_term = 4 * (OWN_TERMS + 2 * walk * OWN_CHUNKS)
        (start,) = meet(
            fields.at[0], 64, edge_lanes(*before, 1, 8), OWN_CHUNKS, [base + 1], edge_term
        )

        def step(k, carry):
            waiting, current = carry
            for odd in (0, 1):
                slot = base + 2 * k + odd
                term = 4 * 3 * OWN_CHUNKS * (FIRST_STEP[walk] + 2 * k + odd)
                behind, here, ahead = meet(
                    block, 64 * odd, span + 8 * k, OWN_CHUNKS, [slot, slot + 1, slot + 2], term
                )
                acc_density[slot] = waiting + behind
                waiting, current = current + here, ahead
            return waiting, current

        waiting, _ = lax.fori_loop(0, pairs, step, (zero, start))
        (end,) = meet(
            fields.at[0],
            0,
            edge_lanes(*after, 1, 8),
            OWN_CHUNKS,
            [base + 2 * pairs],
            edge_term + 4 * OWN_CHUNKS,
        )
        acc_density[base + 2 * pairs] = waiting + end

    own_density(1)
    own_density(2)

    place_in_tile = jnp.bitwise_and(lane, 63).astype(F32)

    def listed_density(walk):
        base, pairs, low, high = WALKS[walk]
        block = theirs.at[walk - 1]

        def member(slot, step):
            lanes = 8 * step + 2 * (walk - 1) + half
            found = zero
            for c in range(LISTED_CHUNKS):
                named = spread(lists_t[pl.ds(8 * c, 8), :], lanes)
                found = found + jnp.where(named == place_in_tile, 1.0, 0.0)
            row_member[pl.ds(slot, 1), :] = total(found)

        def finish(slot, added):
            inside = jnp.broadcast_to(row_member[pl.ds(slot, 1), :], (8, LANES))
            row_density[pl.ds(slot, 1), :] = total(acc_density[slot] + inside * added)

        row_member[pl.ds(base, 1), :] = zero[0:1]
        acc_density[base] = zero

        def step(k, carry):
            waiting, current = carry
            for odd in (0, 1):
                slot = base + 2 * k + odd
                member(slot + 1, 2 * k + odd)
                term = 4 * (OWN_TERMS + EDGE_TERMS) + 4 * 3 * LISTED_CHUNKS * (
                    16 * (walk - 1) + 2 * k + odd
                )
                behind, here, ahead = meet(
                    block,
                    64 * odd,
                    64 * half + 8 * k,
                    LISTED_CHUNKS,
                    [slot, slot + 1, slot + 2],
                    term,
                )
                finish(slot, waiting + behind)
                waiting, current = current + here, ahead
            return waiting, current

        waiting, _ = lax.fori_loop(0, pairs, step, (zero, zero))
        finish(base + 2 * pairs, waiting)

    def to_pairs(rows, walk):
        base, pairs, low, high = WALKS[walk]
        even = rows[pl.ds(base + 1, pairs, stride=2), :]
        odd = rows[pl.ds(base + 2, pairs, stride=2), :]
        return pick_half(even, swap(odd)), pick_half(swap(even), odd)

    for copy in pair_copies[2:]:
        copy.wait_recv()
    theirs[0] = jnp.transpose(incoming[pl.ds(0, 128), :])
    listed_density(1)
    for copy in pair_copies[:2]:
        copy.wait_recv()
    theirs[1] = jnp.transpose(incoming[pl.ds(128, 128), :])
    listed_density(2)
    for walk in (1, 2):
        base, pairs, low, high = WALKS[walk]
        one, two = to_pairs(row_density, walk)
        natural[pl.ds(low, 8), :] = one
        natural[pl.ds(high, 8), :] = two
        for r, rows in ((2 * walk - 2, one), (2 * walk - 1, two)):
            dens_out[r] = spread(rows, picks[pl.ds(8 * r, 8), :])
    dens_copies = [
        send(dens_out.at[r], dens_in.at[r], 6 + r, partners[r]) for r in (3, 2, 1, 0)
    ]

    own_density(0)
    for copy in ghost_copies:
        copy.wait_recv()
    ghosts = theirs_given
    ghosts[...] = jnp.transpose(ghost_in[...])

    def ghost_density(pair, side):
        sums = zero
        aims = [
            jnp.broadcast_to(stack[pl.ds(8 * pair + f, 1), :], (8, LANES)) for f in range(3)
        ]
        at = jnp.zeros((8, LANES), jnp.int32) + 8 * side
        for c in range(OWN_CHUNKS):
            rows = ghosts[pl.ds(8 * c, 8), :]
            dx, dy, dz = [aims[f] - spread(rows, at + f) for f in range(3)]
            near = jnp.maximum(1.0 - (dx * dx + dy * dy + dz * dz), 0.0)
            sums = sums + spread(rows, at + 6) * (near * near * near)
        return sums

    from_lower = jnp.where(dom > 0, ghost_density(0, 0), 0.0)
    from_upper = jnp.where(dom < n_dom - 1, ghost_density(7, 1), 0.0)
    acc_density[1] = acc_density[1] + pick_half(from_lower, zero)
    acc_density[2] = acc_density[2] + pick_half(swap(from_lower), zero)
    acc_density[7] = acc_density[7] + pick_half(zero, swap(from_upper))
    acc_density[8] = acc_density[8] + pick_half(zero, from_upper)
    for slot in range(1, 9):
        row_density[pl.ds(slot, 1), :] = total(acc_density[slot])
    one, two = to_pairs(row_density, 0)
    natural[pl.ds(0, 4), :] = one
    natural[pl.ds(4, 4), :] = two
    density_out[...] = natural[...]

    for slot in (0, 9, 10, 27, 28, 45, 46, 47):
        row_density[pl.ds(slot, 1), :] = zero[0:1] + 1.0
    for at in range(0, SLOTS, 8):
        rho = row_density[pl.ds(at, 8), :]
        sound = jnp.maximum(target[pl.ds(8 * at + 7, 8, stride=8), :], 0.5)
        inverse = 1.0 / rho
        row_a[pl.ds(at, 8), :] = sound - REST * sound * inverse
        row_b[pl.ds(at, 8), :] = 1.0 / (rho * sound)
        row_scale[pl.ds(at, 8), :] = 12.0 * inverse

    def values(rho, sound, mass):
        inverse = 1.0 / rho
        return [sound - REST * sound * inverse, 1.0 / (rho * sound), mass * inverse]

    own_values = []
    for at in range(0, 40, 8):
        own_values.append(
            values(
                natural[pl.ds(at, 8), :],
                stack[pl.ds(8 * at + 7, 8, stride=8), :],
                stack[pl.ds(8 * at + 6, 8, stride=8), :],
            )
        )
    blank = jnp.zeros((32, LANES), F32)
    given[1] = jnp.transpose(
        jnp.concatenate([own_values[n][f] for n in (1, 2, 3, 4) for f in range(3)] + [blank], axis=0)
    )
    for f in range(3):
        extra[pl.ds(16 * f, 8), :] = own_values[0][f]
        extra[pl.ds(16 * f + 8, 1), :] = zero[0:1] + (1.0 if f == 1 else 0.0)
        for place in range(9, 16):
            group, within = divmod(ENTRIES[place], 8)
            extra[pl.ds(16 * f + place, 1), :] = own_values[group][f][within : within + 1]
    extra[pl.ds(48, 80), :] = jnp.zeros((80, LANES), F32)
    given[0] = jnp.transpose(extra[...])

    def push(block, row, lanes, field_stride, chunks, slots, term):
        sums = [[zero, zero, zero] for _ in slots]
        aims = [
            [jnp.broadcast_to(rows[pl.ds(slot, 1), :], (8, LANES)) for rows in (row_a, row_b)]
            for slot in slots
        ]
        for c in range(chunks):
            rows = block[pl.ds(row + 8 * c, 8), :]
            a_source, b_source, gain = [spread(rows, lanes + field_stride * f) for f in range(3)]
            for n in range(len(slots)):
                place = term + 4 * (c * len(slots) + n)
                star = (aims[n][0] + a_source) - terms[place]
                factor = star * (1.0 / (aims[n][1] + b_source)) * gain
                for f in range(3):
                    sums[n][f] = sums[n][f] + factor * terms[place + 1 + f]
        return sums

    def plus(one, two):
        return [a + b for a, b in zip(one, two)]

    zeros = [zero, zero, zero]

    def own_force(walk):
        base, pairs, low, high = WALKS[walk]
        before, after = EDGES[walk]
        span = 4 * half if walk == 0 else 24 * half + 48 * (walk - 1)
        block = given.at[0 if walk == 0 else 1]
        field_stride = 16 if walk == 0 else 8
        edge_term = 4 * (OWN_TERMS + 2 * walk * OWN_CHUNKS)
        (start,) = push(
            given.at[0], 64, edge_lanes(*before, 16, 1), 16, OWN_CHUNKS, [base + 1], edge_term
        )

        def keep(slot, sums):
            for f in range(3):
                acc_force[3 * slot + f] = sums[f]

        def step(k, carry):
            waiting, current = carry
            for odd in (0, 1):
                slot = base + 2 * k + odd
                term = 4 * 3 * OWN_CHUNKS * (FIRST_STEP[walk] + 2 * k + odd)
                behind, here, ahead = push(
                    block,
                    64 * odd,
                    span + k,
                    field_stride,
                    OWN_CHUNKS,
                    [slot, slot + 1, slot + 2],
                    term,
                )
                keep(slot, plus(waiting, behind))
                waiting, current = plus(current, here), ahead
            return waiting, current

        waiting, _ = lax.fori_loop(0, pairs, step, (zeros, start))
        (end,) = push(
            given.at[0],
            0,
            edge_lanes(*after, 16, 1),
            16,
            OWN_CHUNKS,
            [base + 2 * pairs],
            edge_term + 4 * OWN_CHUNKS,
        )
        keep(base + 2 * pairs, plus(waiting, end))

    for walk in range(3):
        own_force(walk)

    for copy in dens_copies:
        copy.wait_recv()
    partner_values = []
    for r in range(4):
        for value in values(
            jnp.maximum(dens_in[r], 0.01),
            jnp.maximum(incoming[pl.ds(64 * r + 7, 8, stride=8), :], 0.5),
            incoming[pl.ds(64 * r + 6, 8, stride=8), :],
        ):
            partner_values.append(value)
    theirs_given[...] = jnp.transpose(jnp.concatenate(partner_values + [blank], axis=0))

    def listed_force(walk):
        base, pairs, low, high = WALKS[walk]

        def finish(slot, added):
            inside = jnp.broadcast_to(row_member[pl.ds(slot, 1), :], (8, LANES))
            scale = row_scale[pl.ds(slot, 1), :]
            for f in range(3):
                sums = total(acc_force[3 * slot + f] + inside * added[f])
                row_force[pl.ds(SLOTS * f + slot, 1), :] = sums * scale

        for f in range(3):
            acc_force[3 * base + f] = zero

        def step(k, carry):
            waiting, current = carry
            for odd in (0, 1):
                slot = base + 2 * k + odd
                term = 4 * (OWN_TERMS + EDGE_TERMS) + 4 * 3 * LISTED_CHUNKS * (
                    16 * (walk - 1) + 2 * k + odd
                )
                behind, here, ahead = push(
                    theirs_given,
                    64 * odd,
                    24 * half + (48 * (walk - 1) + k),
                    8,
                    LISTED_CHUNKS,
                    [slot, slot + 1, slot + 2],
                    term,
                )
                finish(slot, plus(waiting, behind))
                waiting, current = plus(current, here), ahead
            return waiting, current

        waiting, _ = lax.fori_loop(0, pairs, step, (zeros, zeros))
        finish(base + 2 * pairs, waiting)

    for slot in range(1, 9):
        for f in range(3):
            row_force[pl.ds(SLOTS * f + slot, 1), :] = (
                total(acc_force[3 * slot + f]) * row_scale[pl.ds(slot, 1), :]
            )
    listed_force(1)
    listed_force(2)
    for f in range(3):
        for walk in range(3):
            base, pairs, low, high = WALKS[walk]
            one, two = to_pairs(row_force.at[pl.ds(SLOTS * f, SLOTS)], walk)
            accel_out[f, pl.ds(low, pairs), :] = one
            accel_out[f, pl.ds(high, pairs), :] = two
    for copy in pair_copies + ghost_copies + dens_copies:
        copy.wait_send()


def local(particles, ghost_lists, pair_lists):
    vmem = pl.BlockSpec(memory_space=pltpu.VMEM)
    density, accel = pl.pallas_call(
        kernel,
        out_shape=(
            jax.ShapeDtypeStruct((40, LANES), F32),
            jax.ShapeDtypeStruct((3, 40, LANES), F32),
        ),
        in_specs=[vmem, vmem, vmem],
        out_specs=(vmem, vmem),
        scratch_shapes=[
            pltpu.VMEM((320, LANES), F32),
            pltpu.VMEM((8 * SLOTS, LANES), F32),
            pltpu.VMEM((3, 128, LANES), F32),
            pltpu.VMEM((2, 128, LANES), F32),
            pltpu.VMEM((2, 128, LANES), F32),
            pltpu.VMEM((128, LANES), jnp.int32),
            pltpu.VMEM((128, LANES), F32),
            pltpu.VMEM((32, LANES), jnp.int32),
            pltpu.VMEM((4, 64, LANES), F32),
            pltpu.VMEM((256, LANES), F32),
            pltpu.VMEM((2, 8, LANES), F32),
            pltpu.VMEM((128, LANES), F32),
            pltpu.VMEM((4, 8, LANES), F32),
            pltpu.VMEM((4, 8, LANES), F32),
            pltpu.VMEM((4 * TERMS, 8, LANES), F32),
            pltpu.VMEM((SLOTS, 8, LANES), F32),
            pltpu.VMEM((3 * SLOTS, 8, LANES), F32),
            pltpu.VMEM((SLOTS, LANES), F32),
            pltpu.VMEM((SLOTS, LANES), F32),
            pltpu.VMEM((SLOTS, LANES), F32),
            pltpu.VMEM((SLOTS, LANES), F32),
            pltpu.VMEM((SLOTS, LANES), F32),
            pltpu.VMEM((3 * SLOTS, LANES), F32),
            pltpu.VMEM((40, LANES), F32),
            pltpu.VMEM((128, LANES), F32),
            pltpu.VMEM((128, LANES), F32),
            pltpu.SemaphoreType.DMA((10,)),
            pltpu.SemaphoreType.DMA((10,)),
        ],
        compiler_params=pltpu.CompilerParams(
            collective_id=0, has_side_effects=True, vmem_limit_bytes=44 * 1024 * 1024
        ),
    )(particles, ghost_lists, pair_lists)
    return density.reshape(-1), accel.reshape(3, -1)


def solution(mesh):
    in_specs = (P(None, ("grp", "dom")), P(None, ("grp", "dom")), P(None, ("grp", "dom")))
    out_specs = (P(("grp", "dom")), P(None, ("grp", "dom")))
    return jax.shard_map(local, mesh=mesh, in_specs=in_specs, out_specs=out_specs, check_vma=False)
```

```python
import jax
import jax.numpy as jnp
from jax import lax
from jax.experimental import pallas as pl
from jax.experimental.pallas import tpu as pltpu
from jax.sharding import PartitionSpec as P

F32 = jnp.float32
REST = 8.0
FAR = -1000.0
LANES = 128
MESH = pl.DeviceIdType.MESH

WALKS = ((0, 4, 0, 4), (10, 8, 8, 16), (28, 8, 24, 32))
SLOTS = 48
FIRST_STEP = (0, 8, 24)
OWN_CHUNKS = 8
LISTED_CHUNKS = 6
OWN_TERMS = 40 * 3 * OWN_CHUNKS
EDGE_TERMS = 6 * OWN_CHUNKS
LISTED_TERMS = 32 * 3 * LISTED_CHUNKS
TERMS = OWN_TERMS + EDGE_TERMS + LISTED_TERMS

ENTRIES = (0, 1, 2, 3, 4, 5, 6, 7, None, 8, 15, 16, 23, 24, 31, 32)
ENTRY = {pair: place for place, pair in enumerate(ENTRIES)}
EDGES = (((None, 3), (4, 8)), ((7, 15), (16, 24)), ((23, 31), (32, None)))


def spread(rows, lanes):
    return lax.gather(
        rows,
        lanes[:, :, None],
        lax.GatherDimensionNumbers(
            offset_dims=(),
            collapsed_slice_dims=(1,),
            start_index_map=(1,),
            operand_batching_dims=(0,),
            start_indices_batching_dims=(0,),
        ),
        slice_sizes=(1, 1),
        mode=lax.GatherScatterMode.PROMISE_IN_BOUNDS,
    )


def total(block):
    return jnp.sum(block, axis=0, keepdims=True)


def kernel(
    particles_hbm,
    ghost_hbm,
    lists_hbm,
    density_out,
    accel_out,
    particles,
    ghost_lists,
    pair_lists,
    rings,
    stack,
    target,
    fields,
    given,
    theirs,
    lists,
    lists_t,
    picks,
    outgoing,
    incoming,
    ghost_out,
    ghost_in,
    dens_out,
    dens_in,
    terms,
    acc_density,
    acc_force,
    row_density,
    row_a,
    row_b,
    row_scale,
    row_member,
    row_force,
    natural,
    extra,
    theirs_given,
    load_sem,
    send_sem,
    recv_sem,
):
    loads = [
        pltpu.make_async_copy(source, destination, load_sem.at[number])
        for number, (source, destination) in enumerate(
            ((lists_hbm, pair_lists), (particles_hbm, particles), (ghost_hbm, ghost_lists))
        )
    ]
    for load in loads:
        load.start()

    grp = lax.axis_index("grp")
    dom = lax.axis_index("dom")
    n_dom = lax.axis_size("dom")

    def flipped(value, bit):
        return value + bit - 2 * bit * (lax.rem(lax.div(value, bit), 2))

    partners = (
        (grp, flipped(dom, 1)),
        (grp, flipped(dom, 4)),
        (flipped(grp, 1), dom),
        (flipped(grp, 2), dom),
    )
    below = (grp, lax.rem(dom + n_dom - 1, n_dom))
    above = (grp, lax.rem(dom + 1, n_dom))

    barrier = pltpu.get_barrier_semaphore()
    for peer in partners + (below, above):
        pl.semaphore_signal(barrier, inc=1, device_id=peer, device_id_type=MESH)

    lane = lax.broadcasted_iota(jnp.int32, (8, LANES), 1)
    first_half = lane < 64
    half = jnp.where(first_half, 0, 1)

    def pick_half(low, high):
        return jnp.where(first_half[0 : low.shape[0]], low, high)

    def swap(block):
        return pltpu.roll(block, 64, 1)

    loads[0].wait()
    padded = jnp.concatenate([pair_lists[...], jnp.zeros((4, LANES), jnp.int32)], axis=1)
    padded = jnp.concatenate([padded, padded], axis=0)
    for j in range(16):
        lists[pl.ds(8 * j, 8), :] = jnp.bitwise_and(padded[:, 48 * j : 48 * j + LANES], 63)
    for k in range(8):
        even = lists[pl.ds(16 * k, 8), :]
        odd = lists[pl.ds(16 * k + 8, 8), :]
        both = pick_half(even, swap(odd) + 64)
        for r in range(4):
            picks[pl.ds(8 * r + k, 1), :] = both[r : r + 1]

    loads[1].wait()
    loads[2].wait()
    for p in range(40):
        stack[pl.ds(8 * p, 8), :] = particles[:, LANES * p : LANES * p + LANES]

    for r in range(4):
        for k in range(8):
            index = jnp.broadcast_to(picks[pl.ds(8 * r + k, 1), :], (8, LANES))
            outgoing[r, pl.ds(8 * k, 8), :] = spread(stack[pl.ds(8 * (8 + 8 * r + k), 8), :], index)
    faces = jnp.concatenate([ghost_lists[...], ghost_lists[...]], axis=1)
    for side, pair in ((0, 0), (1, 7)):
        index = jnp.broadcast_to(jnp.bitwise_and(faces[side : side + 1], 127), (8, LANES))
        ghost_out[side] = spread(stack[pl.ds(8 * pair, 8), :], index)

    filler_field = lax.broadcasted_iota(jnp.int32, (8, LANES), 0)
    filler = jnp.where(filler_field < 3, FAR, 0.0).astype(F32)
    fields[0] = jnp.transpose(
        jnp.concatenate(
            [filler if pair is None else stack[pl.ds(8 * pair, 8), :] for pair in ENTRIES], axis=0
        )
    )
    fields[1] = jnp.transpose(stack[pl.ds(64, 128), :])
    fields[2] = jnp.transpose(stack[pl.ds(192, 128), :])
    lists_t[...] = jnp.transpose(lists[...].astype(F32))

    zero = jnp.zeros((8, LANES), F32)
    for base, pairs, low, high in WALKS:
        for k in range(pairs):
            one = stack[pl.ds(8 * (low + k), 8), :]
            two = stack[pl.ds(8 * (high + k), 8), :]
            target[pl.ds(8 * (base + 1 + 2 * k), 8), :] = pick_half(one, swap(two))
            target[pl.ds(8 * (base + 2 + 2 * k), 8), :] = pick_half(swap(one), two)
        target[pl.ds(8 * base, 8), :] = zero
        target[pl.ds(8 * (base + 1 + 2 * pairs), 8), :] = zero
    for slot in (46, 47):
        target[pl.ds(8 * slot, 8), :] = zero

    def ahead_of(ring, block, row, lanes, chunks, count, stride=1):
        for f in range(count):
            at = lanes + stride * f
            for c in range(chunks):
                ring[OWN_CHUNKS * f + c] = spread(block[pl.ds(row + 8 * c, 8), :], at)

    def meet(ring, chunks, slots, term):
        sums = [zero for _ in slots]
        aims = [
            [
                jnp.broadcast_to(target[pl.ds(8 * slot + f, 1), :], (8, LANES))
                for f in range(6)
            ]
            for slot in slots
        ]
        for c in range(chunks):
            xs, ys, zs, us, vs, ws, mass = [ring[OWN_CHUNKS * f + c] for f in range(7)]
            for n in range(len(slots)):
                xt, yt, zt, ut, vt, wt = aims[n]
                dx, dy, dz = xt - xs, yt - ys, zt - zs
                squared = dx * dx + dy * dy + dz * dz
                near = jnp.maximum(1.0 - squared, 0.0)
                near2 = near * near
                sums[n] = sums[n] + mass * (near2 * near)
                along = (ut - us) * dx + (vt - vs) * dy + (wt - ws) * dz
                place = term + 4 * (c * len(slots) + n)
                terms[place] = along * lax.rsqrt(jnp.maximum(squared, 0.01))
                terms[place + 1] = near2 * dx
                terms[place + 2] = near2 * dy
                terms[place + 3] = near2 * dz
        return sums

    def edge_lanes(pair_low, pair_high, scale):
        return jnp.where(first_half, scale * ENTRY[pair_low], scale * ENTRY[pair_high])

    def own_density(walk):
        base, pairs, low, high = WALKS[walk]
        before, after = EDGES[walk]
        one, two, edge = rings[3 * (walk % 2) : 3 * (walk % 2) + 3]
        span = half * (32 if walk == 0 else 64)
        edge_term = 4 * (OWN_TERMS + 2 * walk * OWN_CHUNKS)
        ahead_of(edge, fields.at[0], 64, edge_lanes(*before, 8), OWN_CHUNKS, 7)
        ahead_of(one, fields.at[walk], 0, span, OWN_CHUNKS, 7)
        (start,) = meet(edge, OWN_CHUNKS, [base + 1], edge_term)

        def step(k, carry):
            waiting, current = carry
            ahead_of(two, fields.at[walk], 64, span + 8 * k, OWN_CHUNKS, 7)
            for odd in (0, 1):
                slot = base + 2 * k + odd
                term = 4 * 3 * OWN_CHUNKS * (FIRST_STEP[walk] + 2 * k + odd)
                behind, here, ahead = meet(
                    (one, two)[odd], OWN_CHUNKS, [slot, slot + 1, slot + 2], term
                )
                acc_density[slot] = waiting + behind
                waiting, current = current + here, ahead
                if odd == 0:
                    last = k == pairs - 1
                    lanes = jnp.where(last, edge_lanes(*after, 8), span + 8 * (k + 1))
                    block = fields.at[jnp.where(last, 0, walk)]
                    ahead_of(one, block, 0, lanes, OWN_CHUNKS, 7)
            return waiting, current

        waiting, _ = lax.fori_loop(0, pairs, step, (zero, start))
        (end,) = meet(one, OWN_CHUNKS, [base + 2 * pairs], edge_term + 4 * OWN_CHUNKS)
        acc_density[base + 2 * pairs] = waiting + end

    own_density(1)

    pl.semaphore_wait(barrier, 6)

    def send(source, destination, number, peer):
        copy = pltpu.make_async_remote_copy(
            src_ref=source,
            dst_ref=destination,
            send_sem=send_sem.at[number],
            recv_sem=recv_sem.at[number],
            device_id=peer,
            device_id_type=MESH,
        )
        copy.start()
        return copy

    pair_copies = [
        send(outgoing.at[r], incoming.at[pl.ds(64 * r, 64)], r, partners[r]) for r in (3, 2, 1, 0)
    ]
    ghost_copies = [
        send(ghost_out.at[0], ghost_in.at[pl.ds(8, 8)], 4, below),
        send(ghost_out.at[1], ghost_in.at[pl.ds(0, 8)], 5, above),
    ]

    own_density(2)

    place_in_tile = jnp.bitwise_and(lane, 63).astype(F32)

    def listed_density(walk):
        base, pairs, low, high = WALKS[walk]
        block = theirs.at[walk - 1]

        def member(slot, step):
            lanes = 8 * step + 2 * (walk - 1) + half
            found = zero
            for c in range(LISTED_CHUNKS):
                named = spread(lists_t[pl.ds(8 * c, 8), :], lanes)
                found = found + jnp.where(named == place_in_tile, 1.0, 0.0)
            row_member[pl.ds(slot, 1), :] = total(found)

        def finish(slot, added):
            inside = jnp.broadcast_to(row_member[pl.ds(slot, 1), :], (8, LANES))
            row_density[pl.ds(slot, 1), :] = total(acc_density[slot] + inside * added)

        row_member[pl.ds(base, 1), :] = zero[0:1]
        acc_density[base] = zero
        one, two, _ = rings[3 * (walk % 2) : 3 * (walk % 2) + 3]
        ahead_of(one, block, 0, 64 * half, LISTED_CHUNKS, 7)

        def step(k, carry):
            waiting, current = carry
            ahead_of(two, block, 64, 64 * half + 8 * k, LISTED_CHUNKS, 7)
            for odd in (0, 1):
                slot = base + 2 * k + odd
                member(slot + 1, 2 * k + odd)
                term = 4 * (OWN_TERMS + EDGE_TERMS) + 4 * 3 * LISTED_CHUNKS * (
                    16 * (walk - 1) + 2 * k + odd
                )
                behind, here, ahead = meet(
                    (one, two)[odd], LISTED_CHUNKS, [slot, slot + 1, slot + 2], term
                )
                finish(slot, waiting + behind)
                waiting, current = current + here, ahead
                if odd == 0:
                    after = 8 * jnp.minimum(k + 1, pairs - 1)
                    ahead_of(one, block, 0, 64 * half + after, LISTED_CHUNKS, 7)
            return waiting, current

        waiting, _ = lax.fori_loop(0, pairs, step, (zero, zero))
        finish(base + 2 * pairs, waiting)

    def to_pairs(rows, walk):
        base, pairs, low, high = WALKS[walk]
        even = rows[pl.ds(base + 1, pairs, stride=2), :]
        odd = rows[pl.ds(base + 2, pairs, stride=2), :]
        return pick_half(even, swap(odd)), pick_half(swap(even), odd)

    for copy in pair_copies[2:]:
        copy.wait_recv()
    theirs[0] = jnp.transpose(incoming[pl.ds(0, 128), :])
    listed_density(1)
    for copy in pair_copies[:2]:
        copy.wait_recv()
    theirs[1] = jnp.transpose(incoming[pl.ds(128, 128), :])
    listed_density(2)
    for walk in (1, 2):
        base, pairs, low, high = WALKS[walk]
        one, two = to_pairs(row_density, walk)
        natural[pl.ds(low, 8), :] = one
        natural[pl.ds(high, 8), :] = two
        for r, rows in ((2 * walk - 2, one), (2 * walk - 1, two)):
            dens_out[r] = spread(rows, picks[pl.ds(8 * r, 8), :])
    dens_copies = [
        send(dens_out.at[r], dens_in.at[r], 6 + r, partners[r]) for r in (3, 2, 1, 0)
    ]

    own_density(0)
    for copy in ghost_copies:
        copy.wait_recv()
    ghosts = theirs_given
    ghosts[...] = jnp.transpose(ghost_in[...])

    def ghost_density(pair, side):
        sums = zero
        aims = [
            jnp.broadcast_to(stack[pl.ds(8 * pair + f, 1), :], (8, LANES)) for f in range(3)
        ]
        at = jnp.zeros((8, LANES), jnp.int32) + 8 * side
        for c in range(OWN_CHUNKS):
            rows = ghosts[pl.ds(8 * c, 8), :]
            dx, dy, dz = [aims[f] - spread(rows, at + f) for f in range(3)]
            near = jnp.maximum(1.0 - (dx * dx + dy * dy + dz * dz), 0.0)
            sums = sums + spread(rows, at + 6) * (near * near * near)
        return sums

    from_lower = jnp.where(dom > 0, ghost_density(0, 0), 0.0)
    from_upper = jnp.where(dom < n_dom - 1, ghost_density(7, 1), 0.0)
    acc_density[1] = acc_density[1] + pick_half(from_lower, zero)
    acc_density[2] = acc_density[2] + pick_half(swap(from_lower), zero)
    acc_density[7] = acc_density[7] + pick_half(zero, swap(from_upper))
    acc_density[8] = acc_density[8] + pick_half(zero, from_upper)
    for slot in range(1, 9):
        row_density[pl.ds(slot, 1), :] = total(acc_density[slot])
    one, two = to_pairs(row_density, 0)
    natural[pl.ds(0, 4), :] = one
    natural[pl.ds(4, 4), :] = two
    density_out[...] = natural[...]

    for slot in (0, 9, 10, 27, 28, 45, 46, 47):
        row_density[pl.ds(slot, 1), :] = zero[0:1] + 1.0
    for at in range(0, SLOTS, 8):
        rho = row_density[pl.ds(at, 8), :]
        sound = jnp.maximum(target[pl.ds(8 * at + 7, 8, stride=8), :], 0.5)
        inverse = 1.0 / rho
        row_a[pl.ds(at, 8), :] = sound - REST * sound * inverse
        row_b[pl.ds(at, 8), :] = 1.0 / (rho * sound)
        row_scale[pl.ds(at, 8), :] = 12.0 * inverse

    def values(rho, sound, mass):
        inverse = 1.0 / rho
        return [sound - REST * sound * inverse, 1.0 / (rho * sound), mass * inverse]

    own_values = []
    for at in range(0, 40, 8):
        own_values.append(
            values(
                natural[pl.ds(at, 8), :],
                stack[pl.ds(8 * at + 7, 8, stride=8), :],
                stack[pl.ds(8 * at + 6, 8, stride=8), :],
            )
        )
    blank = jnp.zeros((32, LANES), F32)
    given[1] = jnp.transpose(
        jnp.concatenate([own_values[n][f] for n in (1, 2, 3, 4) for f in range(3)] + [blank], axis=0)
    )
    for f in range(3):
        extra[pl.ds(16 * f, 8), :] = own_values[0][f]
        extra[pl.ds(16 * f + 8, 1), :] = zero[0:1] + (1.0 if f == 1 else 0.0)
        for place in range(9, 16):
            group, within = divmod(ENTRIES[place], 8)
            extra[pl.ds(16 * f + place, 1), :] = own_values[group][f][within : within + 1]
    extra[pl.ds(48, 80), :] = jnp.zeros((80, LANES), F32)
    given[0] = jnp.transpose(extra[...])

    def push(ring, chunks, slots, term):
        sums = [[zero, zero, zero] for _ in slots]
        aims = [
            [jnp.broadcast_to(rows[pl.ds(slot, 1), :], (8, LANES)) for rows in (row_a, row_b)]
            for slot in slots
        ]
        for c in range(chunks):
            a_source, b_source, gain = [ring[OWN_CHUNKS * f + c] for f in range(3)]
            for n in range(len(slots)):
                place = term + 4 * (c * len(slots) + n)
                star = (aims[n][0] + a_source) - terms[place]
                factor = star * (1.0 / (aims[n][1] + b_source)) * gain
                for f in range(3):
                    sums[n][f] = sums[n][f] + factor * terms[place + 1 + f]
        return sums

    def plus(one, two):
        return [a + b for a, b in zip(one, two)]

    zeros = [zero, zero, zero]

    def own_force(walk):
        base, pairs, low, high = WALKS[walk]
        before, after = EDGES[walk]
        span = 4 * half if walk == 0 else 24 * half + 48 * (walk - 1)
        block = given.at[0 if walk == 0 else 1]
        field_stride = 16 if walk == 0 else 8
        edge_term = 4 * (OWN_TERMS + 2 * walk * OWN_CHUNKS)
        one, two, edge = rings[3 * (walk % 2) : 3 * (walk % 2) + 3]
        ahead_of(edge, given.at[0], 64, edge_lanes(*before, 1), OWN_CHUNKS, 3, 16)
        ahead_of(one, block, 0, span, OWN_CHUNKS, 3, field_stride)
        (start,) = push(edge, OWN_CHUNKS, [base + 1], edge_term)

        def keep(slot, sums):
            for f in range(3):
                acc_force[3 * slot + f] = sums[f]

        def step(k, carry):
            waiting, current = carry
            ahead_of(two, block, 64, span + k, OWN_CHUNKS, 3, field_stride)
            for odd in (0, 1):
                slot = base + 2 * k + odd
                term = 4 * 3 * OWN_CHUNKS * (FIRST_STEP[walk] + 2 * k + odd)
                behind, here, ahead = push(
                    (one, two)[odd], OWN_CHUNKS, [slot, slot + 1, slot + 2], term
                )
                keep(slot, plus(waiting, behind))
                waiting, current = plus(current, here), ahead
                if odd == 0:
                    after = jnp.minimum(k + 1, pairs - 1)
                    ahead_of(one, block, 0, span + after, OWN_CHUNKS, 3, field_stride)
            return waiting, current

        waiting, _ = lax.fori_loop(0, pairs, step, (zeros, start))
        ahead_of(edge, given.at[0], 0, edge_lanes(*after, 1), OWN_CHUNKS, 3, 16)
        (end,) = push(edge, OWN_CHUNKS, [base + 2 * pairs], edge_term + 4 * OWN_CHUNKS)
        keep(base + 2 * pairs, plus(waiting, end))

    for walk in range(3):
        own_force(walk)

    for copy in dens_copies:
        copy.wait_recv()
    partner_values = []
    for r in range(4):
        for value in values(
            jnp.maximum(dens_in[r], 0.01),
            jnp.maximum(incoming[pl.ds(64 * r + 7, 8, stride=8), :], 0.5),
            incoming[pl.ds(64 * r + 6, 8, stride=8), :],
        ):
            partner_values.append(value)
    theirs_given[...] = jnp.transpose(jnp.concatenate(partner_values + [blank], axis=0))

    def listed_force(walk):
        base, pairs, low, high = WALKS[walk]

        def finish(slot, added):
            inside = jnp.broadcast_to(row_member[pl.ds(slot, 1), :], (8, LANES))
            scale = row_scale[pl.ds(slot, 1), :]
            for f in range(3):
                sums = total(acc_force[3 * slot + f] + inside * added[f])
                row_force[pl.ds(SLOTS * f + slot, 1), :] = sums * scale

        for f in range(3):
            acc_force[3 * base + f] = zero
        one, two, _ = rings[3 * (walk % 2) : 3 * (walk % 2) + 3]
        span = 24 * half + 48 * (walk - 1)
        ahead_of(one, theirs_given, 0, span, LISTED_CHUNKS, 3, 8)

        def step(k, carry):
            waiting, current = carry
            ahead_of(two, theirs_given, 64, span + k, LISTED_CHUNKS, 3, 8)
            for odd in (0, 1):
                slot = base + 2 * k + odd
                term = 4 * (OWN_TERMS + EDGE_TERMS) + 4 * 3 * LISTED_CHUNKS * (
                    16 * (walk - 1) + 2 * k + odd
                )
                behind, here, ahead = push(
                    (one, two)[odd], LISTED_CHUNKS, [slot, slot + 1, slot + 2], term
                )
                finish(slot, plus(waiting, behind))
                waiting, current = plus(current, here), ahead
                if odd == 0:
                    after = jnp.minimum(k + 1, pairs - 1)
                    ahead_of(one, theirs_given, 0, span + after, LISTED_CHUNKS, 3, 8)
            return waiting, current

        waiting, _ = lax.fori_loop(0, pairs, step, (zeros, zeros))
        finish(base + 2 * pairs, waiting)

    for slot in range(1, 9):
        for f in range(3):
            row_force[pl.ds(SLOTS * f + slot, 1), :] = (
                total(acc_force[3 * slot + f]) * row_scale[pl.ds(slot, 1), :]
            )
    listed_force(1)
    listed_force(2)
    for f in range(3):
        for walk in range(3):
            base, pairs, low, high = WALKS[walk]
            one, two = to_pairs(row_force.at[pl.ds(SLOTS * f, SLOTS)], walk)
            accel_out[f, pl.ds(low, pairs), :] = one
            accel_out[f, pl.ds(high, pairs), :] = two
    for copy in pair_copies + ghost_copies + dens_copies:
        copy.wait_send()


def leave(density, accel, density_out, accel_out):
    density_out[...] = density[...]
    for f in range(3):
        for p in range(40):
            accel_out[pl.ds(f, 1), pl.ds(LANES * p, LANES)] = accel[f, pl.ds(p, 1), :]


def local(particles, ghost_lists, pair_lists):
    vmem = pl.BlockSpec(memory_space=pltpu.VMEM)
    hbm = pl.BlockSpec(memory_space=pltpu.HBM)
    density, accel = pl.pallas_call(
        kernel,
        out_shape=(
            jax.ShapeDtypeStruct((40, LANES), F32),
            jax.ShapeDtypeStruct((3, 40, LANES), F32),
        ),
        in_specs=[hbm, hbm, hbm],
        out_specs=(vmem, vmem),
        scratch_shapes=[
            pltpu.VMEM((8, 5120), F32),
            pltpu.VMEM((2, 64), jnp.int32),
            pltpu.VMEM((4, 768), jnp.int32),
            [pltpu.VMEM((7 * OWN_CHUNKS, 8, LANES), F32) for _ in range(6)],
            pltpu.VMEM((320, LANES), F32),
            pltpu.VMEM((8 * SLOTS, LANES), F32),
            pltpu.VMEM((3, 128, LANES), F32),
            pltpu.VMEM((2, 128, LANES), F32),
            pltpu.VMEM((2, 128, LANES), F32),
            pltpu.VMEM((128, LANES), jnp.int32),
            pltpu.VMEM((128, LANES), F32),
            pltpu.VMEM((32, LANES), jnp.int32),
            pltpu.VMEM((4, 64, LANES), F32),
            pltpu.VMEM((256, LANES), F32),
            pltpu.VMEM((2, 8, LANES), F32),
            pltpu.VMEM((128, LANES), F32),
            pltpu.VMEM((4, 8, LANES), F32),
            pltpu.VMEM((4, 8, LANES), F32),
            pltpu.VMEM((4 * TERMS, 8, LANES), F32),
            pltpu.VMEM((SLOTS, 8, LANES), F32),
            pltpu.VMEM((3 * SLOTS, 8, LANES), F32),
            pltpu.VMEM((SLOTS, LANES), F32),
            pltpu.VMEM((SLOTS, LANES), F32),
            pltpu.VMEM((SLOTS, LANES), F32),
            pltpu.VMEM((SLOTS, LANES), F32),
            pltpu.VMEM((SLOTS, LANES), F32),
            pltpu.VMEM((3 * SLOTS, LANES), F32),
            pltpu.VMEM((40, LANES), F32),
            pltpu.VMEM((128, LANES), F32),
            pltpu.VMEM((128, LANES), F32),
            pltpu.SemaphoreType.DMA((3,)),
            pltpu.SemaphoreType.DMA((10,)),
            pltpu.SemaphoreType.DMA((10,)),
        ],
        compiler_params=pltpu.CompilerParams(
            collective_id=0, has_side_effects=True, vmem_limit_bytes=44 * 1024 * 1024
        ),
    )(*[pltpu.with_memory_space_constraint(a, pltpu.HBM) for a in (particles, ghost_lists, pair_lists)])
    density, accel = pl.pallas_call(
        leave,
        out_shape=(
            jax.ShapeDtypeStruct((40, LANES), F32),
            jax.ShapeDtypeStruct((3, 40 * LANES), F32),
        ),
        in_specs=[vmem, vmem],
        out_specs=(vmem, vmem),
    )(density, accel)
    return density.reshape(-1), accel


def solution(mesh):
    in_specs = (P(None, ("grp", "dom")), P(None, ("grp", "dom")), P(None, ("grp", "dom")))
    out_specs = (P(("grp", "dom")), P(None, ("grp", "dom")))
    return jax.shard_map(local, mesh=mesh, in_specs=in_specs, out_specs=out_specs, check_vma=False)
```

```python
import jax
import jax.numpy as jnp
from jax import lax
from jax.experimental import pallas as pl
from jax.experimental.pallas import tpu as pltpu
from jax.sharding import PartitionSpec as P

F32 = jnp.float32
REST = 8.0
FAR = -1000.0
LANES = 128
MESH = pl.DeviceIdType.MESH

WALKS = ((0, 4, 0, 4), (10, 8, 8, 16), (28, 8, 24, 32))
SLOTS = 48
OWN_CHUNKS = 8
LISTED_CHUNKS = 6
BLOCK = 8
OWN_TERMS = BLOCK * 3 * OWN_CHUNKS
LISTED_TERMS = BLOCK * 3 * LISTED_CHUNKS
TERMS = 5 * OWN_TERMS + 4 * LISTED_TERMS

ENTRIES = (0, 1, 2, 3, 4, 5, 6, 7, None, 8, 15, 16, 23, 24, 31, 32)
ENTRY = {pair: place for place, pair in enumerate(ENTRIES)}
EDGES = (((None, 3), (4, 8)), ((7, 15), (16, 24)), ((23, 31), (32, None)))


def spread(rows, lanes):
    return lax.gather(
        rows,
        lanes[:, :, None],
        lax.GatherDimensionNumbers(
            offset_dims=(),
            collapsed_slice_dims=(1,),
            start_index_map=(1,),
            operand_batching_dims=(0,),
            start_indices_batching_dims=(0,),
        ),
        slice_sizes=(1, 1),
        mode=lax.GatherScatterMode.PROMISE_IN_BOUNDS,
    )


def total(block):
    return jnp.sum(block, axis=0, keepdims=True)


def kernel(
    particles_hbm,
    ghost_hbm,
    lists_hbm,
    density_out,
    accel_out,
    particles,
    ghost_lists,
    pair_lists,
    rings,
    stack,
    target,
    fields,
    given,
    theirs,
    lists,
    lists_t,
    picks,
    outgoing,
    incoming,
    ghost_out,
    ghost_in,
    dens_out,
    dens_in,
    terms,
    acc_density,
    acc_force,
    row_density,
    row_a,
    row_b,
    row_scale,
    row_member,
    row_force,
    natural,
    extra,
    theirs_given,
    ghosts,
    load_sem,
    send_sem,
    recv_sem,
):
    loads = [
        pltpu.make_async_copy(source, destination, load_sem.at[number])
        for number, (source, destination) in enumerate(
            ((lists_hbm, pair_lists), (particles_hbm, particles), (ghost_hbm, ghost_lists))
        )
    ]
    for load in loads:
        load.start()

    grp = lax.axis_index("grp")
    dom = lax.axis_index("dom")
    n_dom = lax.axis_size("dom")

    def flipped(value, bit):
        return value + bit - 2 * bit * (lax.rem(lax.div(value, bit), 2))

    partners = (
        (grp, flipped(dom, 1)),
        (grp, flipped(dom, 4)),
        (flipped(grp, 1), dom),
        (flipped(grp, 2), dom),
    )
    below = (grp, lax.rem(dom + n_dom - 1, n_dom))
    above = (grp, lax.rem(dom + 1, n_dom))

    barrier = pltpu.get_barrier_semaphore()
    for peer in partners + (below, above):
        pl.semaphore_signal(barrier, inc=1, device_id=peer, device_id_type=MESH)

    lane = lax.broadcasted_iota(jnp.int32, (8, LANES), 1)
    first_half = lane < 64
    half = jnp.where(first_half, 0, 1)

    def pick_half(low, high):
        return jnp.where(first_half[0 : low.shape[0]], low, high)

    def swap(block):
        return pltpu.roll(block, 64, 1)

    loads[0].wait()
    padded = jnp.concatenate([pair_lists[...], jnp.zeros((4, LANES), jnp.int32)], axis=1)
    padded = jnp.concatenate([padded, padded], axis=0)
    for j in range(16):
        lists[pl.ds(8 * j, 8), :] = jnp.bitwise_and(padded[:, 48 * j : 48 * j + LANES], 63)
    for k in range(8):
        even = lists[pl.ds(16 * k, 8), :]
        odd = lists[pl.ds(16 * k + 8, 8), :]
        both = pick_half(even, swap(odd) + 64)
        for r in range(4):
            picks[pl.ds(8 * r + k, 1), :] = both[r : r + 1]

    loads[1].wait()
    loads[2].wait()
    for p in range(40):
        stack[pl.ds(8 * p, 8), :] = particles[:, LANES * p : LANES * p + LANES]

    filler_field = lax.broadcasted_iota(jnp.int32, (8, LANES), 0)
    filler = jnp.where(filler_field < 3, FAR, 0.0).astype(F32)
    is_listed = jnp.bitwise_and(lane, 63) < 48
    for r in range(4):
        for k in range(8):
            index = jnp.broadcast_to(picks[pl.ds(8 * r + k, 1), :], (8, LANES))
            picked = spread(stack[pl.ds(8 * (8 + 8 * r + k), 8), :], index)
            outgoing[r, pl.ds(8 * k, 8), :] = jnp.where(is_listed, picked, filler)
    faces = jnp.concatenate([ghost_lists[...], ghost_lists[...]], axis=1)
    for side, pair in ((0, 0), (1, 7)):
        index = jnp.broadcast_to(jnp.bitwise_and(faces[side : side + 1], 127), (8, LANES))
        ghost_out[side] = spread(stack[pl.ds(8 * pair, 8), :], index)

    fields[0] = jnp.transpose(
        jnp.concatenate(
            [filler if pair is None else stack[pl.ds(8 * pair, 8), :] for pair in ENTRIES], axis=0
        )
    )
    fields[1] = jnp.transpose(stack[pl.ds(64, 128), :])
    fields[2] = jnp.transpose(stack[pl.ds(192, 128), :])
    lists_t[...] = jnp.transpose(lists[...].astype(F32))

    zero = jnp.zeros((8, LANES), F32)
    for base, pairs, low, high in WALKS:
        for k in range(pairs):
            one = stack[pl.ds(8 * (low + k), 8), :]
            two = stack[pl.ds(8 * (high + k), 8), :]
            target[pl.ds(8 * (base + 1 + 2 * k), 8), :] = pick_half(one, swap(two))
            target[pl.ds(8 * (base + 2 + 2 * k), 8), :] = pick_half(swap(one), two)
        target[pl.ds(8 * base, 8), :] = zero
        target[pl.ds(8 * (base + 1 + 2 * pairs), 8), :] = zero
    for slot in (46, 47):
        target[pl.ds(8 * slot, 8), :] = zero

    def ahead_of(ring, block, row, lanes, chunks, count, stride=1, pace=8):
        for f in range(count):
            at = lanes + stride * f
            for c in range(chunks):
                rows = row + 8 * c if isinstance(row, int) else pl.multiple_of(row + pace * c, 8)
                ring[OWN_CHUNKS * f + c] = spread(block[pl.ds(rows, 8), :], at)

    def meet(ring, chunks, base, near_slots, term, sums):
        aims = [
            [
                jnp.broadcast_to(target[pl.ds(8 * (base + slot) + f, 1), :], (8, LANES))
                for f in range(6)
            ]
            for slot in near_slots
        ]
        for c in range(chunks):
            xs, ys, zs, us, vs, ws, mass = [ring[OWN_CHUNKS * f + c] for f in range(7)]
            for n, slot in enumerate(near_slots):
                xt, yt, zt, ut, vt, wt = aims[n]
                dx, dy, dz = xt - xs, yt - ys, zt - zs
                squared = dx * dx + dy * dy + dz * dz
                near = jnp.maximum(1.0 - squared, 0.0)
                near2 = near * near
                added = mass * (near2 * near)
                sums[slot] = sums[slot] + added if slot in sums else added
                along = (ut - us) * dx + (vt - vs) * dy + (wt - ws) * dz
                place = term + 4 * (c * len(near_slots) + n)
                terms[place] = along * lax.rsqrt(jnp.maximum(squared, 0.01))
                terms[place + 1] = near2 * dx
                terms[place + 2] = near2 * dy
                terms[place + 3] = near2 * dz
        return 4 * chunks * len(near_slots)

    def pattern(one, two):
        return jnp.where(first_half, one, two)

    def choose(b, values):
        result = values[-1]
        for number, value in reversed(list(enumerate(values[:-1]))):
            result = jnp.where(b == number, value, result)
        return result

    before = [(0, ENTRY[one], ENTRY[two]) for (one, two), _ in EDGES]
    after = [(0, ENTRY[one], ENTRY[two]) for _, (one, two) in EDGES]
    first_slots = (1, 11, 19, 29, 37)
    sources = (
        (before[0], (0, 0, 4), after[0]),
        (before[1], (1, 0, 8), (1, 4, 12)),
        ((1, 3, 11), (1, 4, 12), after[1]),
        (before[2], (2, 0, 8), (2, 4, 12)),
        ((2, 3, 11), (2, 4, 12), after[2]),
    )

    def source_of(b, i, table):
        which = 0 if i < 0 else 2 if i >= BLOCK else 1
        return [choose(b, [row[which][n] for row in table]) for n in range(len(table[0][0]))]

    def walked(b, first, stop, fill, each, done):
        sums = {}
        offset = 0
        for i in range(-1, BLOCK + 1):
            if i < BLOCK:
                fill(rings[(i + 2) % len(rings)], b, i + 1)
            else:
                fill(rings[0], jnp.minimum(b + 1, stop - 1), -1)
            near = [t for t in (i - 1, i, i + 1) if 0 <= t < BLOCK]
            offset += each(rings[(i + 1) % len(rings)], near, offset, sums)
            if i >= 1:
                done(i - 1, sums.pop(i - 1))

    def blocks(first, stop, fill, run):
        fill(rings[0], first, -1)

        def body(b, carry):
            run(b)
            return carry

        lax.fori_loop(first, stop, body, 0)

    def own_density(first, stop):
        def fill(ring, b, i):
            block, one, two = source_of(b, i, sources)
            k = i // 2 if 0 <= i < BLOCK else 0
            lanes = pattern(8 * (one + k), 8 * (two + k))
            ahead_of(ring, fields.at[block], 64 * (i % 2), lanes, OWN_CHUNKS, 7)

        def run(b):
            base = choose(b, first_slots)

            def each(ring, near, offset, sums):
                return meet(ring, OWN_CHUNKS, base, near, 4 * OWN_TERMS * b + offset, sums)

            def done(t, total_sum):
                acc_density[base + t] = total_sum

            walked(b, first, stop, fill, each, done)

        blocks(first, stop, fill, run)

    own_density(1, 3)

    pl.semaphore_wait(barrier, 6)

    def send(source, destination, number, peer):
        copy = pltpu.make_async_remote_copy(
            src_ref=source,
            dst_ref=destination,
            send_sem=send_sem.at[number],
            recv_sem=recv_sem.at[number],
            device_id=peer,
            device_id_type=MESH,
        )
        copy.start()
        return copy

    pair_copies = [
        send(outgoing.at[r], incoming.at[pl.ds(64 * r, 64)], r, partners[r]) for r in (3, 2, 1, 0)
    ]
    ghost_copies = [
        send(ghost_out.at[0], ghost_in.at[pl.ds(8, 8)], 4, below),
        send(ghost_out.at[1], ghost_in.at[pl.ds(0, 8)], 5, above),
    ]

    own_density(3, 5)
    own_density(0, 1)

    place_in_tile = jnp.bitwise_and(lane, 63).astype(F32)

    listed_sources = []
    for walk in (0, 1):
        listed_sources.append(((walk, 0, 8, 48, 0), (walk, 0, 8, 0, 8), (walk, 4, 12, 0, 8)))
        listed_sources.append(((walk, 3, 11, 64, 8), (walk, 4, 12, 0, 8), (walk, 4, 12, 48, 0)))

    def listed_density(first, stop):
        def fill(ring, b, i):
            block, one, two, row, pace = source_of(b, i, listed_sources)
            k = i // 2 if 0 <= i < BLOCK else 0
            if 0 <= i < BLOCK:
                row, pace = 64 * (i % 2), 8
            lanes = pattern(8 * (one + k), 8 * (two + k))
            ahead_of(ring, theirs.at[block], row, lanes, LISTED_CHUNKS, 7, pace=pace)

        def run(b):
            base = choose(b, first_slots[1:])

            def each(ring, near, offset, sums):
                term = 4 * (5 * OWN_TERMS + LISTED_TERMS * b) + offset
                return meet(ring, LISTED_CHUNKS, base, near, term, sums)

            def done(t, added):
                slot = base + t
                lanes = choose(b, (0, 64, 2, 66)) + 8 * t
                lanes = pattern(lanes, lanes + 1)
                found = zero
                for c in range(LISTED_CHUNKS):
                    named = spread(lists_t[pl.ds(8 * c, 8), :], lanes)
                    found = found + jnp.where(named == place_in_tile, 1.0, 0.0)
                member = total(found)
                row_member[pl.ds(slot, 1), :] = member
                row_density[pl.ds(slot, 1), :] = total(acc_density[slot] + member * added)

            walked(b, first, stop, fill, each, done)

        blocks(first, stop, fill, run)

    def to_pairs(rows, walk):
        base, pairs, low, high = WALKS[walk]
        even = rows[pl.ds(base + 1, pairs, stride=2), :]
        odd = rows[pl.ds(base + 2, pairs, stride=2), :]
        return pick_half(even, swap(odd)), pick_half(swap(even), odd)

    for copy in ghost_copies:
        copy.wait_recv()
    ghosts[...] = jnp.transpose(ghost_in[...])

    def ghost_density(pair, side):
        sums = zero
        aims = [
            jnp.broadcast_to(stack[pl.ds(8 * pair + f, 1), :], (8, LANES)) for f in range(3)
        ]
        at = jnp.zeros((8, LANES), jnp.int32) + 8 * side
        for c in range(OWN_CHUNKS):
            rows = ghosts[pl.ds(8 * c, 8), :]
            dx, dy, dz = [aims[f] - spread(rows, at + f) for f in range(3)]
            near = jnp.maximum(1.0 - (dx * dx + dy * dy + dz * dz), 0.0)
            sums = sums + spread(rows, at + 6) * (near * near * near)
        return sums

    from_lower = jnp.where(dom > 0, ghost_density(0, 0), 0.0)
    from_upper = jnp.where(dom < n_dom - 1, ghost_density(7, 1), 0.0)
    acc_density[1] = acc_density[1] + pick_half(from_lower, zero)
    acc_density[2] = acc_density[2] + pick_half(swap(from_lower), zero)
    acc_density[7] = acc_density[7] + pick_half(zero, swap(from_upper))
    acc_density[8] = acc_density[8] + pick_half(zero, from_upper)
    for slot in range(1, 9):
        row_density[pl.ds(slot, 1), :] = total(acc_density[slot])

    dens_copies = []
    for walk in (1, 2):
        for r in (2 * walk - 1, 2 * walk - 2):
            pair_copies[3 - r].wait_recv()
        theirs[walk - 1] = jnp.transpose(incoming[pl.ds(128 * (walk - 1), 128), :])
        listed_density(2 * walk - 2, 2 * walk)
        base, pairs, low, high = WALKS[walk]
        one, two = to_pairs(row_density, walk)
        natural[pl.ds(low, 8), :] = one
        natural[pl.ds(high, 8), :] = two
        for r, rows in ((2 * walk - 2, one), (2 * walk - 1, two)):
            dens_out[r] = spread(rows, picks[pl.ds(8 * r, 8), :])
        for r in (2 * walk - 1, 2 * walk - 2):
            dens_copies.append(send(dens_out.at[r], dens_in.at[r], 6 + r, partners[r]))
    one, two = to_pairs(row_density, 0)
    natural[pl.ds(0, 4), :] = one
    natural[pl.ds(4, 4), :] = two

    density_out[...] = natural[...]

    for slot in (0, 9, 10, 27, 28, 45, 46, 47):
        row_density[pl.ds(slot, 1), :] = zero[0:1] + 1.0
    for at in range(0, SLOTS, 8):
        rho = row_density[pl.ds(at, 8), :]
        sound = jnp.maximum(target[pl.ds(8 * at + 7, 8, stride=8), :], 0.5)
        inverse = 1.0 / rho
        row_a[pl.ds(at, 8), :] = sound - REST * sound * inverse
        row_b[pl.ds(at, 8), :] = 1.0 / (rho * sound)
        row_scale[pl.ds(at, 8), :] = 12.0 * inverse

    def values(rho, sound, mass):
        inverse = 1.0 / rho
        return [sound - REST * sound * inverse, 1.0 / (rho * sound), mass * inverse]

    own_values = []
    for at in range(0, 40, 8):
        own_values.append(
            values(
                natural[pl.ds(at, 8), :],
                stack[pl.ds(8 * at + 7, 8, stride=8), :],
                stack[pl.ds(8 * at + 6, 8, stride=8), :],
            )
        )
    blank = jnp.zeros((32, LANES), F32)
    given[1] = jnp.transpose(
        jnp.concatenate([own_values[n][f] for n in (1, 2, 3, 4) for f in range(3)] + [blank], axis=0)
    )
    for f in range(3):
        extra[pl.ds(16 * f, 8), :] = own_values[0][f]
        extra[pl.ds(16 * f + 8, 1), :] = zero[0:1] + (1.0 if f == 1 else 0.0)
        for place in range(9, 16):
            group, within = divmod(ENTRIES[place], 8)
            extra[pl.ds(16 * f + place, 1), :] = own_values[group][f][within : within + 1]
    extra[pl.ds(48, 80), :] = jnp.zeros((80, LANES), F32)
    given[0] = jnp.transpose(extra[...])

    def push(ring, chunks, base, near_slots, term, sums):
        aims = [
            [jnp.broadcast_to(rows[pl.ds(base + slot, 1), :], (8, LANES)) for rows in (row_a, row_b)]
            for slot in near_slots
        ]
        for c in range(chunks):
            a_source, b_source, gain = [ring[OWN_CHUNKS * f + c] for f in range(3)]
            for n, slot in enumerate(near_slots):
                place = term + 4 * (c * len(near_slots) + n)
                star = (aims[n][0] + a_source) - terms[place]
                factor = star * (1.0 / (aims[n][1] + b_source)) * gain
                added = [factor * terms[place + 1 + f] for f in range(3)]
                sums[slot] = [a + b for a, b in zip(sums[slot], added)] if slot in sums else added

        return 4 * chunks * len(near_slots)

    given_sources = []
    for number, row in enumerate(sources):
        shifted = []
        for block, one, two in row:
            if block == 0:
                shifted.append((0, one, two, 16))
            else:
                start = 48 * (block - 1)
                shifted.append((1, start + one, start + 16 + two, 8))
        given_sources.append(tuple(shifted))

    def own_force(first, stop):
        def fill(ring, b, i):
            block, one, two, stride = source_of(b, i, given_sources)
            k = i // 2 if 0 <= i < BLOCK else 0
            ahead_of(
                ring,
                given.at[block],
                64 * (i % 2),
                pattern(one + k, two + k),
                OWN_CHUNKS,
                3,
                stride,
            )

        def run(b):
            base = choose(b, first_slots)

            def each(ring, near, offset, sums):
                return push(ring, OWN_CHUNKS, base, near, 4 * OWN_TERMS * b + offset, sums)

            def done(t, sums):
                for f in range(3):
                    acc_force[3 * (base + t) + f] = sums[f]

            walked(b, first, stop, fill, each, done)

        blocks(first, stop, fill, run)

    own_force(0, 5)
    for slot in range(1, 9):
        for f in range(3):
            row_force[pl.ds(SLOTS * f + slot, 1), :] = (
                total(acc_force[3 * slot + f]) * row_scale[pl.ds(slot, 1), :]
            )

    def listed_force(first, stop):
        def fill(ring, b, i):
            block, one, two, _, _ = source_of(b, i, listed_sources)
            k = i // 2 if 0 <= i < BLOCK else 0
            ahead_of(
                ring,
                theirs_given.at[block],
                64 * (i % 2),
                pattern(one + k, 16 + two + k),
                LISTED_CHUNKS,
                3,
                8,
            )

        def run(b):
            base = choose(b, first_slots[1:])

            def each(ring, near, offset, sums):
                term = 4 * (5 * OWN_TERMS + LISTED_TERMS * b) + offset
                return push(ring, LISTED_CHUNKS, base, near, term, sums)

            def done(t, added):
                slot = base + t
                inside = row_member[pl.ds(slot, 1), :]
                scale = row_scale[pl.ds(slot, 1), :]
                for f in range(3):
                    sums = total(acc_force[3 * slot + f] + inside * added[f])
                    row_force[pl.ds(SLOTS * f + slot, 1), :] = sums * scale

            walked(b, first, stop, fill, each, done)

        blocks(first, stop, fill, run)

    for walk in (1, 2):
        partner_values = []
        for r in (2 * walk - 1, 2 * walk - 2):
            dens_copies[2 * walk - 2 + (2 * walk - 1 - r)].wait_recv()
        for r in (2 * walk - 2, 2 * walk - 1):
            partner_values += values(
                jnp.maximum(dens_in[r], 0.01),
                jnp.maximum(incoming[pl.ds(64 * r + 7, 8, stride=8), :], 0.5),
                incoming[pl.ds(64 * r + 6, 8, stride=8), :],
            )
        rest = [jnp.zeros((80, LANES), F32)]
        theirs_given[walk - 1] = jnp.transpose(jnp.concatenate(partner_values + rest, axis=0))
        listed_force(2 * walk - 2, 2 * walk)
    for f in range(3):
        for walk in range(3):
            base, pairs, low, high = WALKS[walk]
            one, two = to_pairs(row_force.at[pl.ds(SLOTS * f, SLOTS)], walk)
            for k in range(pairs):
                accel_out[pl.ds(f, 1), pl.ds(LANES * (low + k), LANES)] = one[k : k + 1]
                accel_out[pl.ds(f, 1), pl.ds(LANES * (high + k), LANES)] = two[k : k + 1]
    for copy in pair_copies + ghost_copies + dens_copies:
        copy.wait_send()


def leave(density, accel, density_out, accel_out, sem):
    copies = [
        pltpu.make_async_copy(accel, accel_out, sem.at[0]),
        pltpu.make_async_copy(density, density_out, sem.at[1]),
    ]
    for copy in copies:
        copy.start()
    for copy in copies:
        copy.wait()


def local(particles, ghost_lists, pair_lists):
    vmem = pl.BlockSpec(memory_space=pltpu.VMEM)
    hbm = pl.BlockSpec(memory_space=pltpu.HBM)
    density, accel = pl.pallas_call(
        kernel,
        out_shape=(
            pltpu.VMEM((40, LANES), F32),
            pltpu.VMEM((3, 40 * LANES), F32),
        ),
        in_specs=[hbm, hbm, hbm],
        out_specs=(vmem, vmem),
        scratch_shapes=[
            pltpu.VMEM((8, 5120), F32),
            pltpu.VMEM((2, 64), jnp.int32),
            pltpu.VMEM((4, 768), jnp.int32),
            [pltpu.VMEM((7 * OWN_CHUNKS, 8, LANES), F32) for _ in range(5)],
            pltpu.VMEM((320, LANES), F32),
            pltpu.VMEM((8 * SLOTS, LANES), F32),
            pltpu.VMEM((3, 128, LANES), F32),
            pltpu.VMEM((2, 128, LANES), F32),
            pltpu.VMEM((2, 128, LANES), F32),
            pltpu.VMEM((128, LANES), jnp.int32),
            pltpu.VMEM((128, LANES), F32),
            pltpu.VMEM((32, LANES), jnp.int32),
            pltpu.VMEM((4, 64, LANES), F32),
            pltpu.VMEM((256, LANES), F32),
            pltpu.VMEM((2, 8, LANES), F32),
            pltpu.VMEM((128, LANES), F32),
            pltpu.VMEM((4, 8, LANES), F32),
            pltpu.VMEM((4, 8, LANES), F32),
            pltpu.VMEM((4 * TERMS, 8, LANES), F32),
            pltpu.VMEM((SLOTS, 8, LANES), F32),
            pltpu.VMEM((3 * SLOTS, 8, LANES), F32),
            pltpu.VMEM((SLOTS, LANES), F32),
            pltpu.VMEM((SLOTS, LANES), F32),
            pltpu.VMEM((SLOTS, LANES), F32),
            pltpu.VMEM((SLOTS, LANES), F32),
            pltpu.VMEM((SLOTS, LANES), F32),
            pltpu.VMEM((3 * SLOTS, LANES), F32),
            pltpu.VMEM((40, LANES), F32),
            pltpu.VMEM((128, LANES), F32),
            pltpu.VMEM((2, 128, LANES), F32),
            pltpu.VMEM((128, LANES), F32),
            pltpu.SemaphoreType.DMA((3,)),
            pltpu.SemaphoreType.DMA((10,)),
            pltpu.SemaphoreType.DMA((10,)),
        ],
        compiler_params=pltpu.CompilerParams(
            collective_id=0, has_side_effects=True, vmem_limit_bytes=44 * 1024 * 1024
        ),
    )(*[pltpu.with_memory_space_constraint(a, pltpu.HBM) for a in (particles, ghost_lists, pair_lists)])
    density, accel = pl.pallas_call(
        leave,
        out_shape=(
            jax.ShapeDtypeStruct((40, LANES), F32),
            jax.ShapeDtypeStruct((3, 40 * LANES), F32),
        ),
        in_specs=[vmem, vmem],
        out_specs=(hbm, hbm),
        scratch_shapes=[pltpu.SemaphoreType.DMA((2,))],
    )(*[pltpu.with_memory_space_constraint(a, pltpu.VMEM) for a in (density, accel)])
    return density.reshape(-1), accel


def solution(mesh):
    in_specs = (P(None, ("grp", "dom")), P(None, ("grp", "dom")), P(None, ("grp", "dom")))
    out_specs = (P(("grp", "dom")), P(None, ("grp", "dom")))
    return jax.shard_map(local, mesh=mesh, in_specs=in_specs, out_specs=out_specs, check_vma=False)
```

```python
import jax
import jax.numpy as jnp
from jax import lax
from jax.experimental import pallas as pl
from jax.experimental.pallas import tpu as pltpu
from jax.sharding import PartitionSpec as P

F32 = jnp.float32
REST = 8.0
FAR = -1000.0
LANES = 128
MESH = pl.DeviceIdType.MESH

WALKS = ((0, 4, 0, 4), (10, 8, 8, 16), (28, 8, 24, 32))
SLOTS = 48
OWN_CHUNKS = 8
LISTED_CHUNKS = 6
BLOCK = 8
OWN_TERMS = BLOCK * 3 * OWN_CHUNKS
LISTED_TERMS = BLOCK * 3 * LISTED_CHUNKS
TERMS = 5 * OWN_TERMS + 4 * LISTED_TERMS

ENTRIES = (0, 1, 2, 3, 4, 5, 6, 7, None, 8, 15, 16, 23, 24, 31, 32)
ENTRY = {pair: place for place, pair in enumerate(ENTRIES)}
EDGES = (((None, 3), (4, 8)), ((7, 15), (16, 24)), ((23, 31), (32, None)))


def spread(rows, lanes):
    return lax.gather(
        rows,
        lanes[:, :, None],
        lax.GatherDimensionNumbers(
            offset_dims=(),
            collapsed_slice_dims=(1,),
            start_index_map=(1,),
            operand_batching_dims=(0,),
            start_indices_batching_dims=(0,),
        ),
        slice_sizes=(1, 1),
        mode=lax.GatherScatterMode.PROMISE_IN_BOUNDS,
    )


def total(block):
    return jnp.sum(block, axis=0, keepdims=True)


def kernel(
    particles_hbm,
    ghost_hbm,
    lists_hbm,
    density_out,
    accel_out,
    particles,
    ghost_lists,
    pair_lists,
    rings,
    stack,
    target,
    fields,
    given,
    theirs,
    lists,
    lists_t,
    picks,
    outgoing,
    incoming,
    ghost_out,
    ghost_in,
    dens_out,
    dens_in,
    terms,
    acc_density,
    acc_force,
    row_density,
    row_a,
    row_b,
    row_scale,
    row_member,
    row_force,
    natural,
    extra,
    theirs_given,
    ghosts,
    load_sem,
    send_sem,
    recv_sem,
):
    loads = [
        pltpu.make_async_copy(source, destination, load_sem.at[number])
        for number, (source, destination) in enumerate(
            ((lists_hbm, pair_lists), (particles_hbm, particles), (ghost_hbm, ghost_lists))
        )
    ]
    for load in loads:
        load.start()

    grp = lax.axis_index("grp")
    dom = lax.axis_index("dom")
    n_dom = lax.axis_size("dom")

    def flipped(value, bit):
        return value + bit - 2 * bit * (lax.rem(lax.div(value, bit), 2))

    partners = (
        (grp, flipped(dom, 1)),
        (grp, flipped(dom, 4)),
        (flipped(grp, 1), dom),
        (flipped(grp, 2), dom),
    )
    below = (grp, lax.rem(dom + n_dom - 1, n_dom))
    above = (grp, lax.rem(dom + 1, n_dom))

    barrier = pltpu.get_barrier_semaphore()
    for peer in partners + (below, above):
        pl.semaphore_signal(barrier, inc=1, device_id=peer, device_id_type=MESH)

    lane = lax.broadcasted_iota(jnp.int32, (8, LANES), 1)
    first_half = lane < 64
    half = jnp.where(first_half, 0, 1)

    def pick_half(low, high):
        return jnp.where(first_half[0 : low.shape[0]], low, high)

    def swap(block):
        return pltpu.roll(block, 64, 1)

    loads[0].wait()
    padded = jnp.concatenate([pair_lists[...], jnp.zeros((4, LANES), jnp.int32)], axis=1)
    padded = jnp.concatenate([padded, padded], axis=0)
    for j in range(16):
        lists[pl.ds(8 * j, 8), :] = jnp.bitwise_and(padded[:, 48 * j : 48 * j + LANES], 63)
    for k in range(8):
        even = lists[pl.ds(16 * k, 8), :]
        odd = lists[pl.ds(16 * k + 8, 8), :]
        both = pick_half(even, swap(odd) + 64)
        for r in range(4):
            picks[pl.ds(8 * r + k, 1), :] = both[r : r + 1]

    loads[1].wait()
    loads[2].wait()
    for p in range(40):
        stack[pl.ds(8 * p, 8), :] = particles[:, LANES * p : LANES * p + LANES]

    filler_field = lax.broadcasted_iota(jnp.int32, (8, LANES), 0)
    filler = jnp.where(filler_field < 3, FAR, 0.0).astype(F32)
    is_listed = jnp.bitwise_and(lane, 63) < 48
    for r in range(4):
        for k in range(8):
            index = jnp.broadcast_to(picks[pl.ds(8 * r + k, 1), :], (8, LANES))
            picked = spread(stack[pl.ds(8 * (8 + 8 * r + k), 8), :], index)
            outgoing[r, pl.ds(8 * k, 8), :] = jnp.where(is_listed, picked, filler)
    faces = jnp.concatenate([ghost_lists[...], ghost_lists[...]], axis=1)
    for side, pair in ((0, 0), (1, 7)):
        index = jnp.broadcast_to(jnp.bitwise_and(faces[side : side + 1], 127), (8, LANES))
        ghost_out[side] = spread(stack[pl.ds(8 * pair, 8), :], index)

    fields[0] = jnp.transpose(
        jnp.concatenate(
            [filler if pair is None else stack[pl.ds(8 * pair, 8), :] for pair in ENTRIES], axis=0
        )
    )
    fields[1] = jnp.transpose(stack[pl.ds(64, 128), :])

    zero = jnp.zeros((8, LANES), F32)
    for base, pairs, low, high in WALKS:
        for k in range(pairs):
            one = stack[pl.ds(8 * (low + k), 8), :]
            two = stack[pl.ds(8 * (high + k), 8), :]
            target[pl.ds(8 * (base + 1 + 2 * k), 8), :] = pick_half(one, swap(two))
            target[pl.ds(8 * (base + 2 + 2 * k), 8), :] = pick_half(swap(one), two)
        target[pl.ds(8 * base, 8), :] = zero
        target[pl.ds(8 * (base + 1 + 2 * pairs), 8), :] = zero
    for slot in (46, 47):
        target[pl.ds(8 * slot, 8), :] = zero

    def ahead_of(ring, block, row, lanes, chunks, count, stride=1, pace=8):
        for f in range(count):
            at = lanes + stride * f
            for c in range(chunks):
                rows = row + 8 * c if isinstance(row, int) else pl.multiple_of(row + pace * c, 8)
                ring[OWN_CHUNKS * f + c] = spread(block[pl.ds(rows, 8), :], at)

    def meet(ring, chunks, base, near_slots, term, sums):
        aims = [
            [
                jnp.broadcast_to(target[pl.ds(8 * (base + slot) + f, 1), :], (8, LANES))
                for f in range(6)
            ]
            for slot in near_slots
        ]
        for c in range(chunks):
            xs, ys, zs, us, vs, ws, mass = [ring[OWN_CHUNKS * f + c] for f in range(7)]
            for n, slot in enumerate(near_slots):
                xt, yt, zt, ut, vt, wt = aims[n]
                dx, dy, dz = xt - xs, yt - ys, zt - zs
                squared = dx * dx + dy * dy + dz * dz
                near = jnp.maximum(1.0 - squared, 0.0)
                near2 = near * near
                added = mass * (near2 * near)
                sums[slot] = sums[slot] + added if slot in sums else added
                along = (ut - us) * dx + (vt - vs) * dy + (wt - ws) * dz
                place = term + 4 * (c * len(near_slots) + n)
                terms[place] = along * lax.rsqrt(jnp.maximum(squared, 0.01))
                terms[place + 1] = near2 * dx
                terms[place + 2] = near2 * dy
                terms[place + 3] = near2 * dz
        return 4 * chunks * len(near_slots)

    def pattern(one, two):
        return jnp.where(first_half, one, two)

    def choose(b, values):
        result = values[-1]
        for number, value in reversed(list(enumerate(values[:-1]))):
            result = jnp.where(b == number, value, result)
        return result

    before = [(0, ENTRY[one], ENTRY[two]) for (one, two), _ in EDGES]
    after = [(0, ENTRY[one], ENTRY[two]) for _, (one, two) in EDGES]
    first_slots = (1, 11, 19, 29, 37)
    sources = (
        (before[0], (0, 0, 4), after[0]),
        (before[1], (1, 0, 8), (1, 4, 12)),
        ((1, 3, 11), (1, 4, 12), after[1]),
        (before[2], (2, 0, 8), (2, 4, 12)),
        ((2, 3, 11), (2, 4, 12), after[2]),
    )

    def source_of(b, i, table):
        which = 0 if i < 0 else 2 if i >= BLOCK else 1
        return [choose(b, [row[which][n] for row in table]) for n in range(len(table[0][0]))]

    def walked(b, first, stop, fill, each, done):
        sums = {}
        offset = 0
        for i in range(-1, BLOCK + 1):
            if i < BLOCK:
                fill(rings[(i + 2) % len(rings)], b, i + 1)
            else:
                fill(rings[0], jnp.minimum(b + 1, stop - 1), -1)
            near = [t for t in (i - 1, i, i + 1) if 0 <= t < BLOCK]
            offset += each(rings[(i + 1) % len(rings)], near, offset, sums)
            if i >= 1:
                done(i - 1, sums.pop(i - 1))

    def blocks(first, stop, fill, run):
        fill(rings[0], first, -1)

        def body(b, carry):
            run(b)
            return carry

        lax.fori_loop(first, stop, body, 0)

    def own_density(first, stop):
        def fill(ring, b, i):
            block, one, two = source_of(b, i, sources)
            k = i // 2 if 0 <= i < BLOCK else 0
            lanes = pattern(8 * (one + k), 8 * (two + k))
            ahead_of(ring, fields.at[block], 64 * (i % 2), lanes, OWN_CHUNKS, 7)

        def run(b):
            base = choose(b, first_slots)

            def each(ring, near, offset, sums):
                return meet(ring, OWN_CHUNKS, base, near, 4 * OWN_TERMS * b + offset, sums)

            def done(t, total_sum):
                acc_density[base + t] = total_sum

            walked(b, first, stop, fill, each, done)

        blocks(first, stop, fill, run)

    own_density(1, 2)

    pl.semaphore_wait(barrier, 6)

    def send(source, destination, number, peer):
        copy = pltpu.make_async_remote_copy(
            src_ref=source,
            dst_ref=destination,
            send_sem=send_sem.at[number],
            recv_sem=recv_sem.at[number],
            device_id=peer,
            device_id_type=MESH,
        )
        copy.start()
        return copy

    pair_copies = [
        send(outgoing.at[r], incoming.at[pl.ds(64 * r, 64)], r, partners[r]) for r in (3, 2, 1, 0)
    ]
    ghost_copies = [
        send(ghost_out.at[0], ghost_in.at[pl.ds(8, 8)], 4, below),
        send(ghost_out.at[1], ghost_in.at[pl.ds(0, 8)], 5, above),
    ]

    fields[2] = jnp.transpose(stack[pl.ds(192, 128), :])
    lists_t[...] = jnp.transpose(lists[...].astype(F32))

    own_density(2, 5)

    place_in_tile = jnp.bitwise_and(lane, 63).astype(F32)

    listed_sources = []
    for walk in (0, 1):
        listed_sources.append(((walk, 0, 8, 48, 0), (walk, 0, 8, 0, 8), (walk, 4, 12, 0, 8)))
        listed_sources.append(((walk, 3, 11, 64, 8), (walk, 4, 12, 0, 8), (walk, 4, 12, 48, 0)))

    def listed_density(first, stop):
        def fill(ring, b, i):
            block, one, two, row, pace = source_of(b, i, listed_sources)
            k = i // 2 if 0 <= i < BLOCK else 0
            if 0 <= i < BLOCK:
                row, pace = 64 * (i % 2), 8
            lanes = pattern(8 * (one + k), 8 * (two + k))
            ahead_of(ring, theirs.at[block], row, lanes, LISTED_CHUNKS, 7, pace=pace)

        def run(b):
            base = choose(b, first_slots[1:])

            def each(ring, near, offset, sums):
                term = 4 * (5 * OWN_TERMS + LISTED_TERMS * b) + offset
                return meet(ring, LISTED_CHUNKS, base, near, term, sums)

            def done(t, added):
                slot = base + t
                lanes = choose(b, (0, 64, 2, 66)) + 8 * t
                lanes = pattern(lanes, lanes + 1)
                found = zero
                for c in range(LISTED_CHUNKS):
                    named = spread(lists_t[pl.ds(8 * c, 8), :], lanes)
                    found = found + jnp.where(named == place_in_tile, 1.0, 0.0)
                member = total(found)
                row_member[pl.ds(slot, 1), :] = member
                row_density[pl.ds(slot, 1), :] = total(acc_density[slot] + member * added)

            walked(b, first, stop, fill, each, done)

        blocks(first, stop, fill, run)

    def to_pairs(rows, walk):
        base, pairs, low, high = WALKS[walk]
        even = rows[pl.ds(base + 1, pairs, stride=2), :]
        odd = rows[pl.ds(base + 2, pairs, stride=2), :]
        return pick_half(even, swap(odd)), pick_half(swap(even), odd)

    dens_copies = []
    for walk in (1, 2):
        for r in (2 * walk - 1, 2 * walk - 2):
            pair_copies[3 - r].wait_recv()
        theirs[walk - 1] = jnp.transpose(incoming[pl.ds(128 * (walk - 1), 128), :])
        listed_density(2 * walk - 2, 2 * walk)
        base, pairs, low, high = WALKS[walk]
        one, two = to_pairs(row_density, walk)
        natural[pl.ds(low, 8), :] = one
        natural[pl.ds(high, 8), :] = two
        for r, rows in ((2 * walk - 2, one), (2 * walk - 1, two)):
            dens_out[r] = spread(rows, picks[pl.ds(8 * r, 8), :])
        for r in (2 * walk - 1, 2 * walk - 2):
            dens_copies.append(send(dens_out.at[r], dens_in.at[r], 6 + r, partners[r]))
    own_density(0, 1)
    for copy in ghost_copies:
        copy.wait_recv()
    ghosts[...] = jnp.transpose(ghost_in[...])

    def ghost_density(pair, side):
        sums = zero
        aims = [
            jnp.broadcast_to(stack[pl.ds(8 * pair + f, 1), :], (8, LANES)) for f in range(3)
        ]
        at = jnp.zeros((8, LANES), jnp.int32) + 8 * side
        for c in range(OWN_CHUNKS):
            rows = ghosts[pl.ds(8 * c, 8), :]
            dx, dy, dz = [aims[f] - spread(rows, at + f) for f in range(3)]
            near = jnp.maximum(1.0 - (dx * dx + dy * dy + dz * dz), 0.0)
            sums = sums + spread(rows, at + 6) * (near * near * near)
        return sums

    from_lower = jnp.where(dom > 0, ghost_density(0, 0), 0.0)
    from_upper = jnp.where(dom < n_dom - 1, ghost_density(7, 1), 0.0)
    acc_density[1] = acc_density[1] + pick_half(from_lower, zero)
    acc_density[2] = acc_density[2] + pick_half(swap(from_lower), zero)
    acc_density[7] = acc_density[7] + pick_half(zero, swap(from_upper))
    acc_density[8] = acc_density[8] + pick_half(zero, from_upper)
    for slot in range(1, 9):
        row_density[pl.ds(slot, 1), :] = total(acc_density[slot])

    one, two = to_pairs(row_density, 0)
    natural[pl.ds(0, 4), :] = one
    natural[pl.ds(4, 4), :] = two

    density_out[...] = natural[...]

    for slot in (0, 9, 10, 27, 28, 45, 46, 47):
        row_density[pl.ds(slot, 1), :] = zero[0:1] + 1.0
    for at in range(0, SLOTS, 8):
        rho = row_density[pl.ds(at, 8), :]
        sound = jnp.maximum(target[pl.ds(8 * at + 7, 8, stride=8), :], 0.5)
        inverse = 1.0 / rho
        row_a[pl.ds(at, 8), :] = sound - REST * sound * inverse
        row_b[pl.ds(at, 8), :] = 1.0 / (rho * sound)
        row_scale[pl.ds(at, 8), :] = 12.0 * inverse

    def values(rho, sound, mass):
        inverse = 1.0 / rho
        return [sound - REST * sound * inverse, 1.0 / (rho * sound), mass * inverse]

    own_values = []
    for at in range(0, 40, 8):
        own_values.append(
            values(
                natural[pl.ds(at, 8), :],
                stack[pl.ds(8 * at + 7, 8, stride=8), :],
                stack[pl.ds(8 * at + 6, 8, stride=8), :],
            )
        )
    blank = jnp.zeros((32, LANES), F32)
    given[1] = jnp.transpose(
        jnp.concatenate([own_values[n][f] for n in (1, 2, 3, 4) for f in range(3)] + [blank], axis=0)
    )
    for f in range(3):
        extra[pl.ds(16 * f, 8), :] = own_values[0][f]
        extra[pl.ds(16 * f + 8, 1), :] = zero[0:1] + (1.0 if f == 1 else 0.0)
        for place in range(9, 16):
            group, within = divmod(ENTRIES[place], 8)
            extra[pl.ds(16 * f + place, 1), :] = own_values[group][f][within : within + 1]
    extra[pl.ds(48, 80), :] = jnp.zeros((80, LANES), F32)
    given[0] = jnp.transpose(extra[...])

    def push(ring, chunks, base, near_slots, term, sums):
        aims = [
            [jnp.broadcast_to(rows[pl.ds(base + slot, 1), :], (8, LANES)) for rows in (row_a, row_b)]
            for slot in near_slots
        ]
        for c in range(chunks):
            a_source, b_source, gain = [ring[OWN_CHUNKS * f + c] for f in range(3)]
            for n, slot in enumerate(near_slots):
                place = term + 4 * (c * len(near_slots) + n)
                star = (aims[n][0] + a_source) - terms[place]
                factor = star * (1.0 / (aims[n][1] + b_source)) * gain
                added = [factor * terms[place + 1 + f] for f in range(3)]
                sums[slot] = [a + b for a, b in zip(sums[slot], added)] if slot in sums else added

        return 4 * chunks * len(near_slots)

    given_sources = []
    for number, row in enumerate(sources):
        shifted = []
        for block, one, two in row:
            if block == 0:
                shifted.append((0, one, two, 16))
            else:
                start = 48 * (block - 1)
                shifted.append((1, start + one, start + 16 + two, 8))
        given_sources.append(tuple(shifted))

    def own_force(first, stop):
        def fill(ring, b, i):
            block, one, two, stride = source_of(b, i, given_sources)
            k = i // 2 if 0 <= i < BLOCK else 0
            ahead_of(
                ring,
                given.at[block],
                64 * (i % 2),
                pattern(one + k, two + k),
                OWN_CHUNKS,
                3,
                stride,
            )

        def run(b):
            base = choose(b, first_slots)

            def each(ring, near, offset, sums):
                return push(ring, OWN_CHUNKS, base, near, 4 * OWN_TERMS * b + offset, sums)

            def done(t, sums):
                for f in range(3):
                    acc_force[3 * (base + t) + f] = sums[f]

            walked(b, first, stop, fill, each, done)

        blocks(first, stop, fill, run)

    own_force(0, 5)
    for slot in range(1, 9):
        for f in range(3):
            row_force[pl.ds(SLOTS * f + slot, 1), :] = (
                total(acc_force[3 * slot + f]) * row_scale[pl.ds(slot, 1), :]
            )

    def listed_force(first, stop):
        def fill(ring, b, i):
            block, one, two, _, _ = source_of(b, i, listed_sources)
            k = i // 2 if 0 <= i < BLOCK else 0
            ahead_of(
                ring,
                theirs_given.at[block],
                64 * (i % 2),
                pattern(one + k, 16 + two + k),
                LISTED_CHUNKS,
                3,
                8,
            )

        def run(b):
            base = choose(b, first_slots[1:])

            def each(ring, near, offset, sums):
                term = 4 * (5 * OWN_TERMS + LISTED_TERMS * b) + offset
                return push(ring, LISTED_CHUNKS, base, near, term, sums)

            def done(t, added):
                slot = base + t
                inside = row_member[pl.ds(slot, 1), :]
                scale = row_scale[pl.ds(slot, 1), :]
                for f in range(3):
                    sums = total(acc_force[3 * slot + f] + inside * added[f])
                    row_force[pl.ds(SLOTS * f + slot, 1), :] = sums * scale

            walked(b, first, stop, fill, each, done)

        blocks(first, stop, fill, run)

    for walk in (1, 2):
        partner_values = []
        for r in (2 * walk - 1, 2 * walk - 2):
            dens_copies[2 * walk - 2 + (2 * walk - 1 - r)].wait_recv()
        for r in (2 * walk - 2, 2 * walk - 1):
            partner_values += values(
                jnp.maximum(dens_in[r], 0.01),
                jnp.maximum(incoming[pl.ds(64 * r + 7, 8, stride=8), :], 0.5),
                incoming[pl.ds(64 * r + 6, 8, stride=8), :],
            )
        rest = [jnp.zeros((80, LANES), F32)]
        theirs_given[walk - 1] = jnp.transpose(jnp.concatenate(partner_values + rest, axis=0))
        listed_force(2 * walk - 2, 2 * walk)
    for f in range(3):
        for walk in range(3):
            base, pairs, low, high = WALKS[walk]
            one, two = to_pairs(row_force.at[pl.ds(SLOTS * f, SLOTS)], walk)
            for k in range(pairs):
                accel_out[pl.ds(f, 1), pl.ds(LANES * (low + k), LANES)] = one[k : k + 1]
                accel_out[pl.ds(f, 1), pl.ds(LANES * (high + k), LANES)] = two[k : k + 1]
    for copy in pair_copies + ghost_copies + dens_copies:
        copy.wait_send()


def leave(density, accel, density_out, accel_out, sem):
    copies = [
        pltpu.make_async_copy(accel, accel_out, sem.at[0]),
        pltpu.make_async_copy(density, density_out, sem.at[1]),
    ]
    for copy in copies:
        copy.start()
    for copy in copies:
        copy.wait()


def local(particles, ghost_lists, pair_lists):
    vmem = pl.BlockSpec(memory_space=pltpu.VMEM)
    hbm = pl.BlockSpec(memory_space=pltpu.HBM)
    density, accel = pl.pallas_call(
        kernel,
        out_shape=(
            pltpu.VMEM((40, LANES), F32),
            pltpu.VMEM((3, 40 * LANES), F32),
        ),
        in_specs=[hbm, hbm, hbm],
        out_specs=(vmem, vmem),
        scratch_shapes=[
            pltpu.VMEM((8, 5120), F32),
            pltpu.VMEM((2, 64), jnp.int32),
            pltpu.VMEM((4, 768), jnp.int32),
            [pltpu.VMEM((7 * OWN_CHUNKS, 8, LANES), F32) for _ in range(5)],
            pltpu.VMEM((320, LANES), F32),
            pltpu.VMEM((8 * SLOTS, LANES), F32),
            pltpu.VMEM((3, 128, LANES), F32),
            pltpu.VMEM((2, 128, LANES), F32),
            pltpu.VMEM((2, 128, LANES), F32),
            pltpu.VMEM((128, LANES), jnp.int32),
            pltpu.VMEM((128, LANES), F32),
            pltpu.VMEM((32, LANES), jnp.int32),
            pltpu.VMEM((4, 64, LANES), F32),
            pltpu.VMEM((256, LANES), F32),
            pltpu.VMEM((2, 8, LANES), F32),
            pltpu.VMEM((128, LANES), F32),
            pltpu.VMEM((4, 8, LANES), F32),
            pltpu.VMEM((4, 8, LANES), F32),
            pltpu.VMEM((4 * TERMS, 8, LANES), F32),
            pltpu.VMEM((SLOTS, 8, LANES), F32),
            pltpu.VMEM((3 * SLOTS, 8, LANES), F32),
            pltpu.VMEM((SLOTS, LANES), F32),
            pltpu.VMEM((SLOTS, LANES), F32),
            pltpu.VMEM((SLOTS, LANES), F32),
            pltpu.VMEM((SLOTS, LANES), F32),
            pltpu.VMEM((SLOTS, LANES), F32),
            pltpu.VMEM((3 * SLOTS, LANES), F32),
            pltpu.VMEM((40, LANES), F32),
            pltpu.VMEM((128, LANES), F32),
            pltpu.VMEM((2, 128, LANES), F32),
            pltpu.VMEM((128, LANES), F32),
            pltpu.SemaphoreType.DMA((3,)),
            pltpu.SemaphoreType.DMA((10,)),
            pltpu.SemaphoreType.DMA((10,)),
        ],
        compiler_params=pltpu.CompilerParams(
            collective_id=0, has_side_effects=True, vmem_limit_bytes=44 * 1024 * 1024
        ),
    )(*[pltpu.with_memory_space_constraint(a, pltpu.HBM) for a in (particles, ghost_lists, pair_lists)])
    density, accel = pl.pallas_call(
        leave,
        out_shape=(
            jax.ShapeDtypeStruct((40, LANES), F32),
            jax.ShapeDtypeStruct((3, 40 * LANES), F32),
        ),
        in_specs=[vmem, vmem],
        out_specs=(hbm, hbm),
        scratch_shapes=[pltpu.SemaphoreType.DMA((2,))],
    )(*[pltpu.with_memory_space_constraint(a, pltpu.VMEM) for a in (density, accel)])
    return density.reshape(-1), accel


def solution(mesh):
    in_specs = (P(None, ("grp", "dom")), P(None, ("grp", "dom")), P(None, ("grp", "dom")))
    out_specs = (P(("grp", "dom")), P(None, ("grp", "dom")))
    return jax.shard_map(local, mesh=mesh, in_specs=in_specs, out_specs=out_specs, check_vma=False)
```

```python
import jax
import jax.numpy as jnp
from jax import lax
from jax.experimental import pallas as pl
from jax.experimental.pallas import tpu as pltpu
from jax.sharding import PartitionSpec as P

F32 = jnp.float32
REST = 8.0
FAR = -1000.0
LANES = 128
MESH = pl.DeviceIdType.MESH

WALKS = ((0, 4, 0, 4), (10, 8, 8, 16), (28, 8, 24, 32))
SLOTS = 48
OWN_CHUNKS = 8
LISTED_CHUNKS = 6
BLOCK = 8
OWN_TERMS = BLOCK * 3 * OWN_CHUNKS
LISTED_TERMS = BLOCK * 3 * LISTED_CHUNKS
TERMS = 5 * OWN_TERMS + 4 * LISTED_TERMS

ENTRIES = (0, 1, 2, 3, 4, 5, 6, 7, None, 8, 15, 16, 23, 24, 31, 32)
ENTRY = {pair: place for place, pair in enumerate(ENTRIES)}
EDGES = (((None, 3), (4, 8)), ((7, 15), (16, 24)), ((23, 31), (32, None)))


def spread(rows, lanes):
    return lax.gather(
        rows,
        lanes[:, :, None],
        lax.GatherDimensionNumbers(
            offset_dims=(),
            collapsed_slice_dims=(1,),
            start_index_map=(1,),
            operand_batching_dims=(0,),
            start_indices_batching_dims=(0,),
        ),
        slice_sizes=(1, 1),
        mode=lax.GatherScatterMode.PROMISE_IN_BOUNDS,
    )


def total(block):
    return jnp.sum(block, axis=0, keepdims=True)


def kernel(
    particles_hbm,
    ghost_hbm,
    lists_hbm,
    density_out,
    accel_out,
    particles,
    ghost_lists,
    pair_lists,
    rings,
    wide_rings,
    select,
    stack,
    target,
    fields,
    given,
    theirs,
    lists,
    lists_t,
    picks,
    outgoing,
    incoming,
    ghost_out,
    ghost_in,
    dens_out,
    dens_in,
    terms,
    acc_density,
    acc_force,
    row_density,
    row_a,
    row_b,
    row_scale,
    row_member,
    row_force,
    natural,
    extra,
    theirs_given,
    ghosts,
    load_sem,
    send_sem,
    recv_sem,
):
    loads = [
        pltpu.make_async_copy(source, destination, load_sem.at[number])
        for number, (source, destination) in enumerate(
            ((lists_hbm, pair_lists), (particles_hbm, particles), (ghost_hbm, ghost_lists))
        )
    ]
    for load in loads:
        load.start()

    grp = lax.axis_index("grp")
    dom = lax.axis_index("dom")
    n_dom = lax.axis_size("dom")

    def flipped(value, bit):
        return value + bit - 2 * bit * (lax.rem(lax.div(value, bit), 2))

    partners = (
        (grp, flipped(dom, 1)),
        (grp, flipped(dom, 4)),
        (flipped(grp, 1), dom),
        (flipped(grp, 2), dom),
    )
    below = (grp, lax.rem(dom + n_dom - 1, n_dom))
    above = (grp, lax.rem(dom + 1, n_dom))

    barrier = pltpu.get_barrier_semaphore()
    for peer in partners + (below, above):
        pl.semaphore_signal(barrier, inc=1, device_id=peer, device_id_type=MESH)

    lane = lax.broadcasted_iota(jnp.int32, (8, LANES), 1)
    first_half = lane < 64
    half = jnp.where(first_half, 0, 1)

    def pick_half(low, high):
        return jnp.where(first_half[0 : low.shape[0]], low, high)

    def swap(block):
        return pltpu.roll(block, 64, 1)

    loads[0].wait()
    padded = jnp.concatenate([pair_lists[...], jnp.zeros((4, LANES), jnp.int32)], axis=1)
    padded = jnp.concatenate([padded, padded], axis=0)
    for j in range(16):
        lists[pl.ds(8 * j, 8), :] = jnp.bitwise_and(padded[:, 48 * j : 48 * j + LANES], 63)
    for k in range(8):
        even = lists[pl.ds(16 * k, 8), :]
        odd = lists[pl.ds(16 * k + 8, 8), :]
        both = pick_half(even, swap(odd) + 64)
        for r in range(4):
            picks[pl.ds(8 * r + k, 1), :] = both[r : r + 1]

    loads[1].wait()
    loads[2].wait()
    for p in range(40):
        stack[pl.ds(8 * p, 8), :] = particles[:, LANES * p : LANES * p + LANES]

    filler_field = lax.broadcasted_iota(jnp.int32, (8, LANES), 0)
    filler = jnp.where(filler_field < 3, FAR, 0.0).astype(F32)
    for r in range(4):
        for k in range(8):
            index = jnp.broadcast_to(picks[pl.ds(8 * r + k, 1), :], (8, LANES))
            picked = spread(stack[pl.ds(8 * (8 + 8 * r + k), 8), :], index)
            outgoing[r, pl.ds(8 * k, 8), :] = picked
    faces = jnp.concatenate([ghost_lists[...], ghost_lists[...]], axis=1)
    for side, pair in ((0, 0), (1, 7)):
        index = jnp.broadcast_to(jnp.bitwise_and(faces[side : side + 1], 127), (8, LANES))
        ghost_out[side] = spread(stack[pl.ds(8 * pair, 8), :], index)

    wide_row = lax.broadcasted_iota(jnp.int32, (128, 7 * LANES), 0)
    wide_lane = lax.broadcasted_iota(jnp.int32, (128, 7 * LANES), 1)
    for parity in (0, 1):
        wanted = 32 * parity + jnp.where(jnp.bitwise_and(wide_lane, 127) < 64, 0, 64) + wide_lane // LANES
        gap = wide_row - wanted
        chosen = jnp.where((gap == 0) | (gap == 8) | (gap == 16), 1.0, 0.0)
        select[parity] = chosen.astype(jnp.bfloat16)

    def pieces(rows):
        result = []
        for _ in range(3):
            piece = rows.astype(jnp.bfloat16).astype(F32)
            result.append(piece)
            rows = rows - piece
        return result + [jnp.zeros((8, LANES), F32)]

    def standing(blocks_of_rows):
        rows = [piece for rows in blocks_of_rows for piece in pieces(rows)]
        return jnp.transpose(jnp.concatenate(rows, axis=0)).astype(jnp.bfloat16)

    def pair_rows(pair):
        return filler if pair is None else stack[pl.ds(8 * pair, 8), :]

    def stand(walk):
        _, pairs, low, high = WALKS[walk]
        for number in range(pairs // 2):
            four = (low + 2 * number, low + 2 * number + 1, high + 2 * number, high + 2 * number + 1)
            fields[(0, 2, 6)[walk] + number] = standing([pair_rows(pair) for pair in four])
        (low_before, high_before), (low_after, high_after) = EDGES[walk]
        four = (low_after, low_before, high_after, high_before)
        fields[10 + walk] = standing([pair_rows(pair) for pair in four])

    stand(1)

    zero = jnp.zeros((8, LANES), F32)
    for base, pairs, low, high in WALKS:
        for k in range(pairs):
            one = stack[pl.ds(8 * (low + k), 8), :]
            two = stack[pl.ds(8 * (high + k), 8), :]
            target[pl.ds(8 * (base + 1 + 2 * k), 8), :] = pick_half(one, swap(two))
            target[pl.ds(8 * (base + 2 + 2 * k), 8), :] = pick_half(swap(one), two)
        target[pl.ds(8 * base, 8), :] = zero
        target[pl.ds(8 * (base + 1 + 2 * pairs), 8), :] = zero
    for slot in (46, 47):
        target[pl.ds(8 * slot, 8), :] = zero

    def ahead_of(ring, block, row, lanes, chunks, count, stride=1, pace=8):
        for f in range(count):
            at = lanes + stride * f
            for c in range(chunks):
                rows = row + 8 * c if isinstance(row, int) else pl.multiple_of(row + pace * c, 8)
                ring[OWN_CHUNKS * f + c] = spread(block[pl.ds(rows, 8), :], at)

    def widen(ring, block, parity, first, count):
        rows = block[pl.ds(first, count), :]
        for start in range(0, 7, 2):
            width = min(2, 7 - start)
            wide = jnp.dot(
                rows,
                select[parity, :, LANES * start : LANES * (start + width)],
                preferred_element_type=F32,
            )
            for f in range(width):
                for c in range(count // 8):
                    ring[16 * (start + f) + first // 8 + c] = wide[
                        8 * c : 8 * c + 8, LANES * f : LANES * f + LANES
                    ]

    def widen_unit(ring, block, unit):
        if unit == -1:
            widen(ring, block, 1, 64, 64)
        elif unit == 4:
            widen(ring, block, 0, 0, 64)
        else:
            widen(ring, block, unit % 2, 0, 128)

    def walked_wide(b, stop, fill, each, done):
        sums = {}
        offset = 0
        for number, unit in enumerate(range(-1, 5)):
            if unit < 4:
                fill(wide_rings[(number + 1) % 3], b, unit + 1)
            else:
                fill(wide_rings[0], jnp.minimum(b + 1, stop - 1), -1)
            steps = {-1: [(-1, 8)], 4: [(8, 0)]}.get(unit, [(2 * unit, 0), (2 * unit + 1, 8)])
            for i, start in steps:
                near = [t for t in (i - 1, i, i + 1) if 0 <= t < BLOCK]
                offset += each(wide_rings[number % 3], near, offset, sums, start)
                if i >= 1:
                    done(i - 1, sums.pop(i - 1))

    def wide_blocks(first, stop, fill, run):
        fill(wide_rings[0], first, -1)

        def body(b, carry):
            run(b)
            return carry

        lax.fori_loop(first, stop, body, 0)

    def meet(ring, chunks, base, near_slots, term, sums, start):
        aims = [
            [
                jnp.broadcast_to(target[pl.ds(8 * (base + slot) + f, 1), :], (8, LANES))
                for f in range(6)
            ]
            for slot in near_slots
        ]
        for c in range(chunks):
            xs, ys, zs, us, vs, ws, mass = [ring[16 * f + start + c] for f in range(7)]
            for n, slot in enumerate(near_slots):
                xt, yt, zt, ut, vt, wt = aims[n]
                dx, dy, dz = xt - xs, yt - ys, zt - zs
                squared = dx * dx + dy * dy + dz * dz
                near = jnp.maximum(1.0 - squared, 0.0)
                near2 = near * near
                added = mass * (near2 * near)
                sums[slot] = sums[slot] + added if slot in sums else added
                along = (ut - us) * dx + (vt - vs) * dy + (wt - ws) * dz
                place = term + 4 * (c * len(near_slots) + n)
                terms[place] = along * lax.rsqrt(jnp.maximum(squared, 0.01))
                terms[place + 1] = near2 * dx
                terms[place + 2] = near2 * dy
                terms[place + 3] = near2 * dz
        return 4 * chunks * len(near_slots)

    def pattern(one, two):
        return jnp.where(first_half, one, two)

    def choose(b, values):
        result = values[-1]
        for number, value in reversed(list(enumerate(values[:-1]))):
            result = jnp.where(b == number, value, result)
        return result

    before = [(0, ENTRY[one], ENTRY[two]) for (one, two), _ in EDGES]
    after = [(0, ENTRY[one], ENTRY[two]) for _, (one, two) in EDGES]
    first_slots = (1, 11, 19, 29, 37)
    sources = (
        (before[0], (0, 0, 4), after[0]),
        (before[1], (1, 0, 8), (1, 4, 12)),
        ((1, 3, 11), (1, 4, 12), after[1]),
        (before[2], (2, 0, 8), (2, 4, 12)),
        ((2, 3, 11), (2, 4, 12), after[2]),
    )

    def source_of(b, i, table):
        which = 0 if i < 0 else 2 if i >= BLOCK else 1
        return [choose(b, [row[which][n] for row in table]) for n in range(len(table[0][0]))]

    def walked(b, first, stop, fill, each, done):
        sums = {}
        offset = 0
        for i in range(-1, BLOCK + 1):
            if i < BLOCK:
                fill(rings[(i + 2) % len(rings)], b, i + 1)
            else:
                fill(rings[0], jnp.minimum(b + 1, stop - 1), -1)
            near = [t for t in (i - 1, i, i + 1) if 0 <= t < BLOCK]
            offset += each(rings[(i + 1) % len(rings)], near, offset, sums)
            if i >= 1:
                done(i - 1, sums.pop(i - 1))

    def blocks(first, stop, fill, run):
        fill(rings[0], first, -1)

        def body(b, carry):
            run(b)
            return carry

        lax.fori_loop(first, stop, body, 0)

    def own_density(first, stop):
        def fill(ring, b, unit):
            which = {-1: (10, 11, 3, 12, 7), 4: (10, 4, 11, 8, 12)}.get(unit, (0, 2, 4, 6, 8))
            number = choose(b, which) + (unit // 2 if 0 <= unit < 4 else 0)
            widen_unit(ring, fields.at[number], unit)

        def run(b):
            base = choose(b, first_slots)

            def each(ring, near, offset, sums, start):
                return meet(ring, OWN_CHUNKS, base, near, 4 * OWN_TERMS * b + offset, sums, start)

            def done(t, total_sum):
                acc_density[base + t] = total_sum

            walked_wide(b, stop, fill, each, done)

        wide_blocks(first, stop, fill, run)

    own_density(1, 2)

    pl.semaphore_wait(barrier, 6)

    def send(source, destination, number, peer):
        copy = pltpu.make_async_remote_copy(
            src_ref=source,
            dst_ref=destination,
            send_sem=send_sem.at[number],
            recv_sem=recv_sem.at[number],
            device_id=peer,
            device_id_type=MESH,
        )
        copy.start()
        return copy

    pair_copies = [
        send(outgoing.at[r], incoming.at[pl.ds(64 * r, 64)], r, partners[r]) for r in (3, 2, 1, 0)
    ]
    ghost_copies = [
        send(ghost_out.at[0], ghost_in.at[pl.ds(8, 8)], 4, below),
        send(ghost_out.at[1], ghost_in.at[pl.ds(0, 8)], 5, above),
    ]

    stand(2)
    stand(0)
    lists_t[...] = jnp.transpose(lists[...].astype(F32))

    own_density(2, 5)

    place_in_tile = jnp.bitwise_and(lane, 63).astype(F32)

    listed_sources = []
    for walk in (0, 1):
        listed_sources.append(((walk, 0, 8, 48, 0), (walk, 0, 8, 0, 8), (walk, 4, 12, 0, 8)))
        listed_sources.append(((walk, 3, 11, 64, 8), (walk, 4, 12, 0, 8), (walk, 4, 12, 48, 0)))

    def listed_density(first, stop):
        def fill(ring, b, unit):
            which = {-1: (8, 1, 8, 5), 4: (2, 8, 6, 8)}.get(unit, (0, 2, 4, 6))
            number = choose(b, which) + (unit // 2 if 0 <= unit < 4 else 0)
            widen_unit(ring, theirs.at[number], unit)

        def run(b):
            base = choose(b, first_slots[1:])

            def each(ring, near, offset, sums, start):
                term = 4 * (5 * OWN_TERMS + LISTED_TERMS * b) + offset
                return meet(ring, LISTED_CHUNKS, base, near, term, sums, start)

            def done(t, added):
                slot = base + t
                lanes = choose(b, (0, 64, 2, 66)) + 8 * t
                lanes = pattern(lanes, lanes + 1)
                found = zero
                for c in range(LISTED_CHUNKS):
                    named = spread(lists_t[pl.ds(8 * c, 8), :], lanes)
                    found = found + jnp.where(named == place_in_tile, 1.0, 0.0)
                member = total(found)
                row_member[pl.ds(slot, 1), :] = member
                row_density[pl.ds(slot, 1), :] = total(acc_density[slot] + member * added)

            walked_wide(b, stop, fill, each, done)

        wide_blocks(first, stop, fill, run)

    def to_pairs(rows, walk):
        base, pairs, low, high = WALKS[walk]
        even = rows[pl.ds(base + 1, pairs, stride=2), :]
        odd = rows[pl.ds(base + 2, pairs, stride=2), :]
        return pick_half(even, swap(odd)), pick_half(swap(even), odd)

    theirs[8] = standing([filler] * 4)
    dens_copies = []
    for walk in (1, 2):
        for r in (2 * walk - 1, 2 * walk - 2):
            pair_copies[3 - r].wait_recv()
        for number in range(4):
            starts = [128 * (walk - 1) + at + 16 * number for at in (0, 8, 64, 72)]
            theirs[4 * (walk - 1) + number] = standing([incoming[pl.ds(at, 8), :] for at in starts])
        listed_density(2 * walk - 2, 2 * walk)
        base, pairs, low, high = WALKS[walk]
        one, two = to_pairs(row_density, walk)
        natural[pl.ds(low, 8), :] = one
        natural[pl.ds(high, 8), :] = two
        for r, rows in ((2 * walk - 2, one), (2 * walk - 1, two)):
            dens_out[r] = spread(rows, picks[pl.ds(8 * r, 8), :])
        for r in (2 * walk - 1, 2 * walk - 2):
            dens_copies.append(send(dens_out.at[r], dens_in.at[r], 6 + r, partners[r]))
    own_density(0, 1)
    for copy in ghost_copies:
        copy.wait_recv()
    ghosts[...] = jnp.transpose(ghost_in[...])

    def ghost_density(pair, side):
        sums = zero
        aims = [
            jnp.broadcast_to(stack[pl.ds(8 * pair + f, 1), :], (8, LANES)) for f in range(3)
        ]
        at = jnp.zeros((8, LANES), jnp.int32) + 8 * side
        for c in range(OWN_CHUNKS):
            rows = ghosts[pl.ds(8 * c, 8), :]
            dx, dy, dz = [aims[f] - spread(rows, at + f) for f in range(3)]
            near = jnp.maximum(1.0 - (dx * dx + dy * dy + dz * dz), 0.0)
            sums = sums + spread(rows, at + 6) * (near * near * near)
        return sums

    from_lower = jnp.where(dom > 0, ghost_density(0, 0), 0.0)
    from_upper = jnp.where(dom < n_dom - 1, ghost_density(7, 1), 0.0)
    acc_density[1] = acc_density[1] + pick_half(from_lower, zero)
    acc_density[2] = acc_density[2] + pick_half(swap(from_lower), zero)
    acc_density[7] = acc_density[7] + pick_half(zero, swap(from_upper))
    acc_density[8] = acc_density[8] + pick_half(zero, from_upper)
    for slot in range(1, 9):
        row_density[pl.ds(slot, 1), :] = total(acc_density[slot])

    one, two = to_pairs(row_density, 0)
    natural[pl.ds(0, 4), :] = one
    natural[pl.ds(4, 4), :] = two

    density_out[...] = natural[...]

    for slot in (0, 9, 10, 27, 28, 45, 46, 47):
        row_density[pl.ds(slot, 1), :] = zero[0:1] + 1.0
    for at in range(0, SLOTS, 8):
        rho = row_density[pl.ds(at, 8), :]
        sound = jnp.maximum(target[pl.ds(8 * at + 7, 8, stride=8), :], 0.5)
        inverse = 1.0 / rho
        row_a[pl.ds(at, 8), :] = sound - REST * sound * inverse
        row_b[pl.ds(at, 8), :] = 1.0 / (rho * sound)
        row_scale[pl.ds(at, 8), :] = 12.0 * inverse

    def values(rho, sound, mass):
        inverse = 1.0 / rho
        return [sound - REST * sound * inverse, 1.0 / (rho * sound), mass * inverse]

    own_values = []
    for at in range(0, 40, 8):
        own_values.append(
            values(
                natural[pl.ds(at, 8), :],
                stack[pl.ds(8 * at + 7, 8, stride=8), :],
                stack[pl.ds(8 * at + 6, 8, stride=8), :],
            )
        )
    blank = jnp.zeros((32, LANES), F32)
    given[1] = jnp.transpose(
        jnp.concatenate([own_values[n][f] for n in (1, 2, 3, 4) for f in range(3)] + [blank], axis=0)
    )
    for f in range(3):
        extra[pl.ds(16 * f, 8), :] = own_values[0][f]
        extra[pl.ds(16 * f + 8, 1), :] = zero[0:1] + (1.0 if f == 1 else 0.0)
        for place in range(9, 16):
            group, within = divmod(ENTRIES[place], 8)
            extra[pl.ds(16 * f + place, 1), :] = own_values[group][f][within : within + 1]
    extra[pl.ds(48, 80), :] = jnp.zeros((80, LANES), F32)
    given[0] = jnp.transpose(extra[...])

    def push(ring, chunks, base, near_slots, term, sums):
        aims = [
            [jnp.broadcast_to(rows[pl.ds(base + slot, 1), :], (8, LANES)) for rows in (row_a, row_b)]
            for slot in near_slots
        ]
        for c in range(chunks):
            a_source, b_source, gain = [ring[OWN_CHUNKS * f + c] for f in range(3)]
            for n, slot in enumerate(near_slots):
                place = term + 4 * (c * len(near_slots) + n)
                star = (aims[n][0] + a_source) - terms[place]
                factor = star * (1.0 / (aims[n][1] + b_source)) * gain
                added = [factor * terms[place + 1 + f] for f in range(3)]
                sums[slot] = [a + b for a, b in zip(sums[slot], added)] if slot in sums else added

        return 4 * chunks * len(near_slots)

    given_sources = []
    for number, row in enumerate(sources):
        shifted = []
        for block, one, two in row:
            if block == 0:
                shifted.append((0, one, two, 16))
            else:
                start = 48 * (block - 1)
                shifted.append((1, start + one, start + 16 + two, 8))
        given_sources.append(tuple(shifted))

    def own_force(first, stop):
        def fill(ring, b, i):
            block, one, two, stride = source_of(b, i, given_sources)
            k = i // 2 if 0 <= i < BLOCK else 0
            ahead_of(
                ring,
                given.at[block],
                64 * (i % 2),
                pattern(one + k, two + k),
                OWN_CHUNKS,
                3,
                stride,
            )

        def run(b):
            base = choose(b, first_slots)

            def each(ring, near, offset, sums):
                return push(ring, OWN_CHUNKS, base, near, 4 * OWN_TERMS * b + offset, sums)

            def done(t, sums):
                for f in range(3):
                    acc_force[3 * (base + t) + f] = sums[f]

            walked(b, first, stop, fill, each, done)

        blocks(first, stop, fill, run)

    own_force(0, 5)
    for slot in range(1, 9):
        for f in range(3):
            row_force[pl.ds(SLOTS * f + slot, 1), :] = (
                total(acc_force[3 * slot + f]) * row_scale[pl.ds(slot, 1), :]
            )

    def listed_force(first, stop):
        def fill(ring, b, i):
            block, one, two, _, _ = source_of(b, i, listed_sources)
            k = i // 2 if 0 <= i < BLOCK else 0
            ahead_of(
                ring,
                theirs_given.at[block],
                64 * (i % 2),
                pattern(one + k, 16 + two + k),
                LISTED_CHUNKS,
                3,
                8,
            )

        def run(b):
            base = choose(b, first_slots[1:])

            def each(ring, near, offset, sums):
                term = 4 * (5 * OWN_TERMS + LISTED_TERMS * b) + offset
                return push(ring, LISTED_CHUNKS, base, near, term, sums)

            def done(t, added):
                slot = base + t
                inside = row_member[pl.ds(slot, 1), :]
                scale = row_scale[pl.ds(slot, 1), :]
                for f in range(3):
                    sums = total(acc_force[3 * slot + f] + inside * added[f])
                    row_force[pl.ds(SLOTS * f + slot, 1), :] = sums * scale

            walked(b, first, stop, fill, each, done)

        blocks(first, stop, fill, run)

    for walk in (1, 2):
        partner_values = []
        for r in (2 * walk - 1, 2 * walk - 2):
            dens_copies[2 * walk - 2 + (2 * walk - 1 - r)].wait_recv()
        for r in (2 * walk - 2, 2 * walk - 1):
            partner_values += values(
                jnp.maximum(dens_in[r], 0.01),
                jnp.maximum(incoming[pl.ds(64 * r + 7, 8, stride=8), :], 0.5),
                incoming[pl.ds(64 * r + 6, 8, stride=8), :],
            )
        rest = [jnp.zeros((80, LANES), F32)]
        theirs_given[walk - 1] = jnp.transpose(jnp.concatenate(partner_values + rest, axis=0))
        listed_force(2 * walk - 2, 2 * walk)
    for f in range(3):
        for walk in range(3):
            base, pairs, low, high = WALKS[walk]
            one, two = to_pairs(row_force.at[pl.ds(SLOTS * f, SLOTS)], walk)
            for k in range(pairs):
                accel_out[pl.ds(f, 1), pl.ds(LANES * (low + k), LANES)] = one[k : k + 1]
                accel_out[pl.ds(f, 1), pl.ds(LANES * (high + k), LANES)] = two[k : k + 1]
    for copy in pair_copies + ghost_copies + dens_copies:
        copy.wait_send()


def leave(density, accel, density_out, accel_out, sem):
    copies = [
        pltpu.make_async_copy(accel, accel_out, sem.at[0]),
        pltpu.make_async_copy(density, density_out, sem.at[1]),
    ]
    for copy in copies:
        copy.start()
    for copy in copies:
        copy.wait()


def local(particles, ghost_lists, pair_lists):
    vmem = pl.BlockSpec(memory_space=pltpu.VMEM)
    hbm = pl.BlockSpec(memory_space=pltpu.HBM)
    density, accel = pl.pallas_call(
        kernel,
        out_shape=(
            pltpu.VMEM((40, LANES), F32),
            pltpu.VMEM((3, 40 * LANES), F32),
        ),
        in_specs=[hbm, hbm, hbm],
        out_specs=(vmem, vmem),
        scratch_shapes=[
            pltpu.VMEM((8, 5120), F32),
            pltpu.VMEM((2, 64), jnp.int32),
            pltpu.VMEM((4, 768), jnp.int32),
            [pltpu.VMEM((3 * OWN_CHUNKS, 8, LANES), F32) for _ in range(5)],
            [pltpu.VMEM((7 * 16, 8, LANES), F32) for _ in range(3)],
            pltpu.VMEM((2, 128, 7 * LANES), jnp.bfloat16),
            pltpu.VMEM((320, LANES), F32),
            pltpu.VMEM((8 * SLOTS, LANES), F32),
            pltpu.VMEM((13, 128, LANES), jnp.bfloat16),
            pltpu.VMEM((2, 128, LANES), F32),
            pltpu.VMEM((9, 128, LANES), jnp.bfloat16),
            pltpu.VMEM((128, LANES), jnp.int32),
            pltpu.VMEM((128, LANES), F32),
            pltpu.VMEM((32, LANES), jnp.int32),
            pltpu.VMEM((4, 64, LANES), F32),
            pltpu.VMEM((256, LANES), F32),
            pltpu.VMEM((2, 8, LANES), F32),
            pltpu.VMEM((128, LANES), F32),
            pltpu.VMEM((4, 8, LANES), F32),
            pltpu.VMEM((4, 8, LANES), F32),
            pltpu.VMEM((4 * TERMS, 8, LANES), F32),
            pltpu.VMEM((SLOTS, 8, LANES), F32),
            pltpu.VMEM((3 * SLOTS, 8, LANES), F32),
            pltpu.VMEM((SLOTS, LANES), F32),
            pltpu.VMEM((SLOTS, LANES), F32),
            pltpu.VMEM((SLOTS, LANES), F32),
            pltpu.VMEM((SLOTS, LANES), F32),
            pltpu.VMEM((SLOTS, LANES), F32),
            pltpu.VMEM((3 * SLOTS, LANES), F32),
            pltpu.VMEM((40, LANES), F32),
            pltpu.VMEM((128, LANES), F32),
            pltpu.VMEM((2, 128, LANES), F32),
            pltpu.VMEM((128, LANES), F32),
            pltpu.SemaphoreType.DMA((3,)),
            pltpu.SemaphoreType.DMA((10,)),
            pltpu.SemaphoreType.DMA((10,)),
        ],
        compiler_params=pltpu.CompilerParams(
            collective_id=0, has_side_effects=True, vmem_limit_bytes=44 * 1024 * 1024
        ),
    )(*[pltpu.with_memory_space_constraint(a, pltpu.HBM) for a in (particles, ghost_lists, pair_lists)])
    density, accel = pl.pallas_call(
        leave,
        out_shape=(
            jax.ShapeDtypeStruct((40, LANES), F32),
            jax.ShapeDtypeStruct((3, 40 * LANES), F32),
        ),
        in_specs=[vmem, vmem],
        out_specs=(hbm, hbm),
        scratch_shapes=[pltpu.SemaphoreType.DMA((2,))],
    )(*[pltpu.with_memory_space_constraint(a, pltpu.VMEM) for a in (density, accel)])
    return density.reshape(-1), accel


def solution(mesh):
    in_specs = (P(None, ("grp", "dom")), P(None, ("grp", "dom")), P(None, ("grp", "dom")))
    out_specs = (P(("grp", "dom")), P(None, ("grp", "dom")))
    return jax.shard_map(local, mesh=mesh, in_specs=in_specs, out_specs=out_specs, check_vma=False)
```
